128 devices in a mesh: pt: 32 (over x, y, core), var: 4 (over z).
Axes of the slice: x: 4, y: 4, z: 4, core: 2. Of those that a mesh axis runs over, the one named last changes fastest.
Arguments:
- green_tensor: bfloat16 [6, 2, 1024, 1024], P(None, None, ('pt', 'var')), may hold values from -0.0078125 to 0.0078125
- moment: bfloat16 [6, 1024], P(None, ('pt', 'var')), may hold values from -6 to 6
- slip_rate: bfloat16 [64, 1024, 1024], P('var', 'pt'), may hold values from -6 to 6
- owner_shard: int32 [1024, 1], P('pt'), may hold values from 0 to 31; in each aligned block of 32 rows (0 to 31, 32 to 63, ...) at most 2 rows name the same one
- point_slot: int32 [1024], P('pt'), may hold values from 0 to 31
- live_counts: int32 [32], P('pt'), may hold values from 1 to 32, 768 in all
Outputs:
- seismograms: float32 [64, 2, 1024], P('var', None, 'pt')
The draws below stay inside these ranges and needn't reach their ends.
Inputs may be any that keep to these rules, and one draw needn't show every extreme that they name: `owner_shard`: within each aligned block of 32 rows (the rows of one index of pt), no value is named by more than 2 rows; some block names one value exactly 2 times. `live_counts`: the counts sum to 768 and one of them equals 32.
All inputs are finite; a program needn't handle non-finite values. No bound on the sum of `live_counts` on one device may be relied on, other than what follows from the above.
Results may differ from the reference program's by a relative error of at most 0.0029.
Values may be sent and summed in bfloat16 or wider, within the bound.
A program may use at most 256 MiB of HBM per device.

```python
import math
import jax
import jax.numpy as jnp
import numpy as np
from jax import lax

R_DEV = 32
NT = 1024
CAP = 2
POINTS = 1024
ROWS = 1024
VARS = 64
NSHARD = 32
N_PT = 32


def with_ends(entries, key, least, largest):
    longest = entries.shape.index(max(entries.shape))
    spots = []
    for shift in (0, 1):
        where = [jax.random.randint(jax.random.fold_in(key, axis), (), 0, length) for axis, length in enumerate(entries.shape)]
        where[longest] = (where[longest] + shift) % entries.shape[longest]
        spots.append(tuple(where))
    return entries.at[spots[0]].set(least).at[spots[1]].set(largest)


def level_of(stream_key, shape, cuts, least, top_value):
    gain = 1.0
    for axis_at, shards_of in cuts:
        draws = jax.random.uniform(jax.random.fold_in(jax.random.fold_in(stream_key, 6), axis_at), (shards_of,), jnp.float32, least / len(cuts), top_value / len(cuts))
        gain = gain * jnp.repeat(jnp.exp(draws), shape[axis_at] // shards_of).reshape((-1,) + (1,) * (len(shape) - 1 - axis_at))
    return gain


def split_up(amount, total, limit, skew):
    portions = [(1 << 20) // math.isqrt(standing ** skew) + 1 for standing in range(2, amount + 1)]
    surplus, holding = total - limit - (amount - 1), [1] * (amount - 1)
    while surplus > 0:
        free = [i for i in range(amount - 1) if holding[i] < limit]
        mass, budget = sum([portions[i] for i in free]), surplus
        for i in free:
            more = min(limit - holding[i], max(1, budget * portions[i] // mass), surplus)
            holding[i] = holding[i] + more
            surplus = surplus - more
    return np.array([limit] + holding)


def uneven(stream_key, number_of, total, bound, lean):
    if number_of == 2:
        one = jax.random.randint(stream_key, (), max(1, total - bound), min(bound, total - 1) + 1)
        return jnp.stack([one, total - one])
    sizes = jnp.asarray(split_up(number_of, total, bound, lean), jnp.int32)
    twos = (number_of - 1) // 2
    giver, receiver = sizes[1:1 + 2 * twos:2], sizes[2:2 + 2 * twos:2]
    margin = jnp.minimum(giver - 1, bound - receiver)
    moved = jax.random.randint(jax.random.fold_in(stream_key, 1), (twos,), 0, 1 << 20) % (margin + 1)
    sizes = sizes.at[1:1 + 2 * twos:2].set(giver - moved).at[2:2 + 2 * twos:2].set(receiver + moved)
    return sizes[jax.random.permutation(jax.random.fold_in(stream_key, 2), number_of)]


def shared_out(rng, own, number, rows, number_of, top, reach, skew):
    ranking = jax.random.permutation(rng, number_of)
    packed, usual = portions_of(number_of, rows * top, reach, skew, True), portions_of(number_of, rows * top, reach, skew, False)
    places = jnp.arange(number_of)

    def named(tallies, rotation):
        used = int((tallies > 0).sum())
        fixed = max(1, used // 4)
        moved = fixed + (places - fixed + rotation * (used - fixed)) % max(1, number_of - fixed)
        return jnp.zeros((number_of,), jnp.int32).at[ranking[jnp.where(places < fixed, places, moved)]].set(jnp.asarray(tallies, jnp.int32))

    tallies = jnp.where(number % 4 == 0, named(packed, number // 4), named(usual, number - number // 4 - 1))
    mixed = jax.random.permutation(jax.random.fold_in(own, 3), number_of)
    giver, sink = mixed[0:number_of // 2 * 2:2], mixed[1:number_of // 2 * 2:2]
    margin = jnp.minimum(tallies[giver] - 1, reach - tallies[sink]) // 2
    margin = jnp.where((giver == ranking[0]) | (sink == ranking[0]) | (tallies[sink] == 0), 0, jnp.maximum(margin, 0))
    moved = jax.random.randint(jax.random.fold_in(own, 4), (number_of // 2,), 0, 1 << 20) % (margin + 1)
    tallies = tallies.at[giver].add(-moved).at[sink].add(moved)
    labels = jnp.searchsorted(jnp.cumsum(tallies), jnp.arange(rows * top), side="right").astype(jnp.int32)
    grid = labels.reshape(top, rows).T
    grid = grid[jax.random.permutation(jax.random.fold_in(own, 1), rows)]
    rotation = jax.random.randint(jax.random.fold_in(own, 2), (rows, 1), 0, top)
    return jnp.take_along_axis(grid, (jnp.arange(top)[None, :] + rotation) % top, axis=1)


def portions_of(number_of, total, reach, lean, full):
    loads = [(1 << 20) // math.isqrt(rank ** lean) + 1 for rank in range(1, number_of + 1)]
    largest = reach if full else min(reach, max(-(-total // number_of), total * loads[0] // sum(loads)))
    least = 1 if total - largest >= number_of - 1 else 0
    holding, spare = [largest] + [least] * (number_of - 1), total - largest - least * (number_of - 1)
    while spare > 0:
        movable = [i for i in range(1, number_of) if holding[i] < largest] or [i for i in range(1, number_of) if holding[i] < reach]
        whole, budget = sum([loads[i] for i in movable]), spare
        for i in movable:
            more = min(reach - holding[i], max(1, budget * loads[i] // whole), spare)
            holding[i] = holding[i] + more
            spare = spare - more
    return np.array(holding)


def scatter_about(key, shape, deviation, most, pieces=(), kind=jnp.bfloat16):
    result = deviation * jax.random.normal(key, shape, jnp.float32)
    if pieces:
        result = result * level_of(key, shape, pieces, -0.22, 0.18)
    return jnp.clip(result, -most, most).astype(kind)


def setup_inputs(seed: int = 0) -> dict:
    keys = jax.random.split(jax.random.key(seed), 7)
    green_tensor = scatter_about(keys[0], (6, 2, POINTS, NT), (R_DEV * N_PT * NT // 2) ** -0.5, 0.0078125, ((2, 128),))
    moment = scatter_about(keys[1], (6, POINTS), 0.4, 6.0, ((1, 128),))
    slip_rate = scatter_about(keys[2], (VARS, ROWS, NT), 1.0, 6.0, ((0, 4), (1, 32)))
    owner_shard_keys = jax.random.split(jax.random.fold_in(keys[3], 1), ROWS // R_DEV)
    owner_shard_turns = jax.random.permutation(jax.random.fold_in(keys[3], 3), ROWS // R_DEV)
    owner_shard = jax.vmap(lambda own, number: shared_out(jax.random.fold_in(keys[3], 2), own, number, R_DEV, N_PT, 1, CAP, 2))(owner_shard_keys, owner_shard_turns).reshape((ROWS, 1))
    point_slot = with_ends(jax.random.randint(keys[4], (ROWS,), 0, R_DEV), jax.random.fold_in(keys[4], 1), 0, R_DEV - 1).astype(jnp.int32)
    live_counts = uneven(keys[5], NSHARD, 3 * R_DEV * N_PT // 4, R_DEV, 2).astype(jnp.int32)
    return {"green_tensor": green_tensor, "moment": moment, "slip_rate": slip_rate, "owner_shard": owner_shard, "point_slot": point_slot, "live_counts": live_counts}


def reference(green_tensor, moment, slip_rate, owner_shard, point_slot, live_counts):
    green_field = jnp.sum(moment.astype(jnp.float32)[:, None, :, None] * green_tensor.astype(jnp.float32), axis=0).astype(jnp.bfloat16)
    target = owner_shard[:, 0].astype(jnp.int32) * R_DEV + point_slot.astype(jnp.int32)
    within = jnp.arange(ROWS, dtype=jnp.int32) % R_DEV
    limits = jnp.repeat(live_counts.astype(jnp.int32), R_DEV, total_repeat_length=ROWS)
    live_rows = (within < limits).astype(jnp.float32)
    selected = jnp.take(green_field, target, axis=1).astype(jnp.float32) * live_rows[None, :, None]
    spectra = jnp.fft.rfft(selected, n=2 * NT, axis=-1)

    def single(series):
        source = jnp.fft.rfft(series.astype(jnp.float32), n=2 * NT, axis=-1)
        summed = jnp.einsum('hrf,rf->hf', spectra, source)
        return jnp.fft.irfft(summed, n=2 * NT, axis=-1)[:, :NT].astype(jnp.float32)

    return lax.map(single, slip_rate)
```

```python
import functools

import jax
import jax.numpy as jnp
from jax import lax
from jax.experimental import pallas as pl
from jax.experimental.pallas import tpu as pltpu
from jax.sharding import PartitionSpec as P

F32 = jnp.float32
BF16 = jnp.bfloat16
LANES = 128
N_PT = 32
N_VAR = 4
HELD = 32
OWN = 8
BLOCKS = 8
VARS = 16
MESH = pl.DeviceIdType.MESH


def request_table(owner_ref, slot_ref):
    row = lax.broadcasted_iota(jnp.int32, (N_PT, LANES), 0)
    lane = lax.broadcasted_iota(jnp.int32, (N_PT, LANES), 1)
    table = jnp.zeros((N_PT, LANES), jnp.int32)
    count = jnp.zeros((N_PT, LANES), jnp.int32)
    for r in range(HELD):
        hit = row == owner_ref[r, 0]
        table = jnp.where(hit & (lane == count), slot_ref[r], table)
        count = count + hit.astype(jnp.int32)
    return table


def kernel(
    slip_hbm, green_hbm, moment_ref, owner_ref, slot_ref, live_ref, out_ref,
    slip, green, fold, field, ask, asked, asked_s, pick_s, outbox, inbox,
    gathered, xmat, gmat, zmat, part, landed,
    slip_sem, green_sem, ask_sem, z_send, z_recv, q_send, q_recv, g_send, g_recv, y_send, y_recv,
):
    me = lax.axis_index("pt")
    level = lax.axis_index("var")

    slip_copy = pltpu.make_async_copy(slip_hbm, slip, slip_sem)
    green_copy = pltpu.make_async_copy(green_hbm, green, green_sem)
    green_copy.start()
    slip_copy.start()

    barrier = pltpu.get_barrier_semaphore()

    def greet(k, carry):
        pl.semaphore_signal(barrier, inc=1, device_id={"pt": lax.rem(me + k, N_PT)}, device_id_type=MESH)
        return carry

    lax.fori_loop(1, N_PT, greet, 0)
    for d in range(1, N_VAR):
        pl.semaphore_signal(barrier, inc=1, device_id={"var": lax.rem(level + d, N_VAR)}, device_id_type=MESH)

    table = request_table(owner_ref, slot_ref)
    for o in range(N_PT):
        ask[o] = table[o : o + 1, :]
    seen = jnp.int32(0)
    for r in range(HELD):
        owner = owner_ref[r, 0]
        bit = jnp.left_shift(jnp.int32(1), owner)
        second = jnp.where((seen & bit) != 0, 1, 0)
        seen = seen | bit
        place = lax.rem(me + (2 * N_PT - 1) - owner, N_PT)
        pick_s[r] = jnp.where(r < live_ref[0], 2 * place + second, 2 * N_PT)

    green_copy.wait()
    tall = jnp.transpose(moment_ref[...].astype(F32))
    tall = jnp.concatenate([tall, tall], axis=0)
    for m in range(BLOCKS):
        total = jnp.zeros((2 * OWN, LANES), F32)
        for c in range(6):
            total = total + tall[:, c : c + 1] * green[16 * c : 16 * c + 16, LANES * m : LANES * (m + 1)].astype(F32)
        fold[16 * m : 16 * m + 16, :] = total
    for p in range(OWN):
        one = jnp.concatenate(
            [fold[pl.ds(p, BLOCKS, stride=16), :], fold[pl.ds(8 + p, BLOCKS, stride=16), :]], axis=0
        )
        field[level * OWN + p] = one.astype(BF16)

    pl.semaphore_wait(barrier, N_PT - 1 + N_VAR - 1)

    for d in range(1, N_VAR):
        pltpu.make_async_remote_copy(
            src_ref=field.at[pl.ds(level * OWN, OWN)],
            dst_ref=field.at[pl.ds(level * OWN, OWN)],
            send_sem=z_send.at[d - 1],
            recv_sem=z_recv.at[d - 1],
            device_id={"var": lax.rem(level + d, N_VAR)},
            device_id_type=MESH,
        ).start()

    def send_ask(k, carry):
        other = lax.rem(me + k, N_PT)
        pltpu.make_async_remote_copy(
            src_ref=ask.at[other],
            dst_ref=asked.at[k - 1],
            send_sem=q_send,
            recv_sem=q_recv,
            device_id={"pt": other},
            device_id_type=MESH,
        ).start()
        return carry

    lax.fori_loop(1, N_PT, send_ask, 0)
    asked[N_PT - 1] = ask[me]

    slip_copy.wait()
    lane16 = lax.broadcasted_iota(jnp.int32, (16, LANES), 1) // 32

    def turn(g, carry):
        for n in range(BLOCKS):
            piece = slip[pl.ds(4 * g, 4), :, LANES * n : LANES * (n + 1)].reshape(LANES, LANES)
            flipped = jnp.transpose(piece)
            for half in range(2):
                rows = [flipped[16 * (4 * half + q) : 16 * (4 * half + q) + 16, :] for q in range(4)]
                for v in range(4):
                    mixed = rows[v]
                    for q in range(4):
                        if q != v:
                            mixed = jnp.where(lane16 == q, pltpu.roll(rows[q], 32 * ((q - v) % 4), 1), mixed)
                    xmat[
                        pl.ds(pl.multiple_of((4 * g + v) * 16, 16), 16),
                        256 * (BLOCKS - 1 - n) + LANES * half : 256 * (BLOCKS - 1 - n) + LANES * (half + 1),
                    ] = mixed
        return carry

    lax.fori_loop(0, 4, turn, 0)

    everyone = pltpu.make_async_remote_copy(
        src_ref=ask.at[pl.ds(0, N_PT - 1)], dst_ref=asked.at[pl.ds(0, N_PT - 1)], send_sem=q_send, recv_sem=q_recv,
        device_id={"pt": lax.rem(me + 1, N_PT)}, device_id_type=MESH,
    )
    everyone.wait_recv()
    to_scalar = pltpu.make_async_copy(asked, asked_s, ask_sem)
    to_scalar.start()
    for d in range(1, N_VAR):
        source = lax.rem(level + (N_VAR - d), N_VAR)
        pltpu.make_async_remote_copy(
            src_ref=field.at[pl.ds(level * OWN, OWN)],
            dst_ref=field.at[pl.ds(source * OWN, OWN)],
            send_sem=z_send.at[d - 1],
            recv_sem=z_recv.at[d - 1],
            device_id={"var": lax.rem(level + d, N_VAR)},
            device_id_type=MESH,
        ).wait()
    to_scalar.wait()

    def serve(k, carry):
        other = lax.rem(me + k, N_PT)
        for s in range(2):
            outbox[2 * (k - 1) + s] = field[asked_s[N_PT - 1 - k, 0, s]]
        pltpu.make_async_remote_copy(
            src_ref=outbox.at[pl.ds(2 * (k - 1), 2)],
            dst_ref=inbox.at[pl.ds(2 * (k - 1), 2)],
            send_sem=g_send,
            recv_sem=g_recv,
            device_id={"pt": other},
            device_id_type=MESH,
        ).start()
        return carry

    lax.fori_loop(1, N_PT, serve, 0)
    for s in range(2):
        inbox[2 * (N_PT - 1) + s] = field[asked_s[N_PT - 1, 0, s]]
    inbox[2 * N_PT] = jnp.zeros((16, LANES), BF16)

    boxes = pltpu.make_async_remote_copy(
        src_ref=outbox.at[pl.ds(0, 2 * (N_PT - 1))], dst_ref=inbox.at[pl.ds(0, 2 * (N_PT - 1))],
        send_sem=g_send, recv_sem=g_recv, device_id={"pt": lax.rem(me + 1, N_PT)}, device_id_type=MESH,
    )
    boxes.wait_recv()
    everyone.wait_send()

    for r in range(HELD):
        gathered[16 * r : 16 * r + 16, :] = inbox[pick_s[r]].astype(F32)
    lane32 = lax.broadcasted_iota(jnp.int32, (HELD, LANES), 1)
    for h in range(2):
        before = None
        for m in range(BLOCKS):
            here = gathered[pl.ds(BLOCKS * h + m, HELD, stride=16), :].astype(BF16)
            for c in range(BLOCKS):
                if c == 0:
                    delayed = here
                else:
                    now = pltpu.roll(here, 16 * c, 1)
                    then = jnp.zeros_like(now) if before is None else pltpu.roll(before, 16 * c, 1)
                    delayed = jnp.where(lane32 >= 16 * c, now, then)
                gmat[256 * m + 32 * c : 256 * m + 32 * c + 32, LANES * h : LANES * (h + 1)] = delayed
            before = here

    wide = lax.broadcasted_iota(jnp.int32, (VARS, 2 * LANES), 1) % LANES
    group8 = lax.broadcasted_iota(jnp.int32, (8, LANES), 1) // 32
    spill = jnp.zeros((VARS, 2 * LANES), F32)
    for m in range(BLOCKS):
        product = jnp.dot(
            xmat[:, 256 * (BLOCKS - 1 - m) :], gmat[: 256 * (m + 1), :], preferred_element_type=F32
        )
        zmat[m % 2, 0] = product[:, :LANES]
        zmat[m % 2, 1] = product[:, LANES:]
        total = spill
        spill = jnp.zeros((VARS, 2 * LANES), F32)
        for f in range(16):
            rows = [zmat[m % 2, h, pl.ds(f, VARS, stride=16), :] for h in range(2)]
            if f == 0:
                total = total + jnp.concatenate(rows, axis=1)
            else:
                rolled = jnp.concatenate([pltpu.roll(rows[h], f, 1) for h in range(2)], axis=1)
                kept = jnp.where(wide >= f, rolled, 0.0)
                total = total + kept
                spill = spill + (rolled - kept)
        quarters = [total[8 * (q // 2) : 8 * (q // 2) + 8, LANES * (q % 2) : LANES * (q % 2) + LANES] for q in range(4)]
        for t in range(4):
            mixed = quarters[t]
            for q in range(4):
                if q != t:
                    mixed = jnp.where(group8 == q, pltpu.roll(quarters[q], 32 * ((q - t) % 4), 1), mixed)
            part[4 * m + t] = mixed

    def hand_out(k, carry):
        other = lax.rem(me + k, N_PT)
        pltpu.make_async_remote_copy(
            src_ref=part.at[other],
            dst_ref=landed.at[k - 1],
            send_sem=y_send,
            recv_sem=y_recv,
            device_id={"pt": other},
            device_id_type=MESH,
        ).start()
        return carry

    lax.fori_loop(1, N_PT, hand_out, 0)
    mine = part[me]
    boxes.wait_send()
    parts = pltpu.make_async_remote_copy(
        src_ref=part.at[pl.ds(0, N_PT - 1)], dst_ref=landed.at[pl.ds(0, N_PT - 1)],
        send_sem=y_send, recv_sem=y_recv, device_id={"pt": lax.rem(me + 1, N_PT)}, device_id_type=MESH,
    )
    parts.wait_recv()
    out_ref[...] = mine + jnp.sum(landed[...], axis=0)
    parts.wait_send()


def on_device(green_tensor, moment, slip_rate, owner_shard, point_slot, live_counts):
    hbm = pl.BlockSpec(memory_space=pl.ANY)
    vmem = pl.BlockSpec(memory_space=pltpu.VMEM)
    smem = pl.BlockSpec(memory_space=pltpu.SMEM)
    dma = pltpu.SemaphoreType.DMA
    length = slip_rate.shape[2]
    packed = pl.pallas_call(
        kernel,
        out_shape=jax.ShapeDtypeStruct((8, LANES), F32),
        in_specs=[hbm, hbm, vmem, smem, smem, smem],
        out_specs=vmem,
        scratch_shapes=[
            pltpu.VMEM((VARS, HELD, length), BF16),
            pltpu.VMEM((96, length), BF16),
            pltpu.VMEM((LANES, LANES), F32),
            pltpu.VMEM((HELD, 16, LANES), BF16),
            pltpu.VMEM((N_PT, 1, LANES), jnp.int32),
            pltpu.VMEM((N_PT, 1, LANES), jnp.int32),
            pltpu.SMEM((N_PT, 1, LANES), jnp.int32),
            pltpu.SMEM((HELD,), jnp.int32),
            pltpu.VMEM((2 * (N_PT - 1), 16, LANES), BF16),
            pltpu.VMEM((2 * N_PT + 1, 16, LANES), BF16),
            pltpu.VMEM((HELD * 16, LANES), F32),
            pltpu.VMEM((VARS * 16, 256 * BLOCKS), BF16),
            pltpu.VMEM((256 * BLOCKS, 2 * LANES), BF16),
            pltpu.VMEM((2, 2, VARS * 16, LANES), F32),
            pltpu.VMEM((N_PT, 8, LANES), F32),
            pltpu.VMEM((N_PT - 1, 8, LANES), F32),
            dma, dma, dma, dma((N_VAR - 1,)), dma((N_VAR - 1,)), dma, dma, dma, dma, dma, dma,
        ],
        compiler_params=pltpu.CompilerParams(
            collective_id=0, has_side_effects=True, vmem_limit_bytes=32 * 1024 * 1024
        ),
        name="synthesis",
    )(slip_rate, green_tensor.reshape(96, length), moment, owner_shard, point_slot, live_counts)
    return packed.reshape(8, 2, 2, 32).transpose(1, 0, 2, 3).reshape(VARS, 2, 32)


def solution(mesh):
    in_specs = (
        P(None, None, ("pt", "var"), None),
        P(None, ("pt", "var")),
        P("var", "pt", None),
        P("pt", None),
        P("pt"),
        P("pt"),
    )
    out_specs = P("var", None, "pt")
    return jax.shard_map(on_device, mesh=mesh, in_specs=in_specs, out_specs=out_specs, check_vma=False)
```

```python
import functools

import jax
import jax.numpy as jnp
from jax import lax
from jax.experimental import pallas as pl
from jax.experimental.pallas import tpu as pltpu
from jax.sharding import PartitionSpec as P

F32 = jnp.float32
BF16 = jnp.bfloat16
LANES = 128
N_PT = 32
N_VAR = 4
HELD = 32
OWN = 8
BLOCKS = 8
VARS = 16
MESH = pl.DeviceIdType.MESH


def each_offset(body):
    def odd(q):
        return 1 + 2 * lax.rem(q, 2)

    def run(count, pair):
        def step(i, carry):
            dx, dy = pair(lax.div(i, 2))
            body(dx, dy, lax.rem(i, 2))
            return carry

        lax.fori_loop(0, count, step, 0)

    run(2, lambda q: (2, 2))
    run(8, lambda q: (2 + lax.div(q, 2) * (odd(q) - 2), odd(q) + lax.div(q, 2) * (2 - odd(q))))
    run(8, lambda q: (1 + 2 * lax.div(q, 2), odd(q)))
    run(4, lambda q: (2 * lax.rem(q, 2), 2 - 2 * lax.rem(q, 2)))
    run(8, lambda q: (lax.div(q, 2) * odd(q), (1 - lax.div(q, 2)) * odd(q)))
    body(0, 0, 1)


def code(dx, dy, dc):
    return lax.rem(8 * dx + 2 * dy + dc + N_PT - 1, N_PT)


def request_table(owner_ref, slot_ref):
    row = lax.broadcasted_iota(jnp.int32, (N_PT, LANES), 0)
    lane = lax.broadcasted_iota(jnp.int32, (N_PT, LANES), 1)
    table = jnp.zeros((N_PT, LANES), jnp.int32)
    count = jnp.zeros((N_PT, LANES), jnp.int32)
    for r in range(HELD):
        hit = row == owner_ref[0, r]
        table = jnp.where(hit & (lane == count), slot_ref[r], table)
        count = count + hit.astype(jnp.int32)
    return table


def kernel(
    slip_hbm, green_hbm, moment_hbm, owner_hbm, slot_hbm, live_ref, out_ref,
    slip, green, moment, owner_ref, slot_ref, fold, field, ask, asked_v, asked, pick_s, second_s, field32, outbox, inbox_0, inbox_1,
    gathered, xmat, gmat, zmat, part, landed,
    slip_sem, green_sem, small_sem, ask_sem, z_send, z_recv, q_send, q_recv, g_send, g_recv, y_send, y_recv,
):
    me = lax.axis_index("pt")
    level = lax.axis_index("var")
    at_x, at_y, at_c = lax.div(me, 8), lax.rem(lax.div(me, 2), 4), lax.rem(me, 2)

    def peer(dx, dy, dc):
        return 8 * lax.rem(at_x + dx, 4) + 2 * lax.rem(at_y + dy, 4) + lax.rem(at_c + dc, 2)

    def above(d):
        return {"var": lax.rem(level + d, N_VAR)}

    sibling = {"pt": peer(0, 0, 1)}

    slip_copy = pltpu.make_async_copy(slip_hbm, slip, slip_sem)
    green_copy = pltpu.make_async_copy(green_hbm, green, green_sem)
    small = [
        pltpu.make_async_copy(source, here, small_sem.at[i])
        for i, (source, here) in enumerate(
            [(owner_hbm, owner_ref), (slot_hbm, slot_ref), (moment_hbm, moment)]
        )
    ]
    for one in small:
        one.start()
    green_copy.start()
    slip_copy.start()

    barrier = pltpu.get_barrier_semaphore()

    def greet(dx, dy, dc):
        pl.semaphore_signal(barrier, inc=1, device_id={"pt": peer(dx, dy, dc)}, device_id_type=MESH)

    each_offset(greet)
    for d in range(1, N_VAR):
        pl.semaphore_signal(barrier, inc=1, device_id=above(d), device_id_type=MESH)

    for one in small:
        one.wait()
    table = request_table(owner_ref, slot_ref)
    for o in range(N_PT):
        ask[o] = table[o : o + 1, :]
    seen = jnp.int32(0)
    for r in range(HELD):
        owner = owner_ref[0, r]
        bit = jnp.left_shift(jnp.int32(1), owner)
        second = jnp.where((seen & bit) != 0, 1, 0)
        seen = seen | bit
        place = (
            8 * lax.rem(at_x + 4 - lax.div(owner, 8), 4)
            + 2 * lax.rem(at_y + 4 - lax.rem(lax.div(owner, 2), 4), 4)
            + lax.rem(at_c + lax.rem(owner, 2), 2)
        )
        place = lax.rem(place + N_PT - 1, N_PT)
        pick_s[r] = jnp.where(r < live_ref[0], place, N_PT)
        second_s[r] = second

    green_copy.wait()
    tall = jnp.transpose(moment[...].astype(F32))
    tall = jnp.concatenate([tall, tall], axis=0)
    for m in range(BLOCKS):
        total = jnp.zeros((2 * OWN, LANES), F32)
        for c in range(6):
            total = total + tall[:, c : c + 1] * green[16 * c : 16 * c + 16, LANES * m : LANES * (m + 1)].astype(F32)
        for h in range(2):
            row = OWN * (8 * (m // 4) + 4 * h + m % 4)
            fold[row : row + OWN, :] = total[OWN * h : OWN * h + OWN]
    for p in range(OWN):
        one = jnp.concatenate([fold[pl.ds(p, 8, stride=OWN), :], fold[pl.ds(64 + p, 8, stride=OWN), :]], axis=0)
        field[level * OWN + p] = one.astype(BF16)

    pl.semaphore_wait(barrier, N_PT - 1 + N_VAR - 1)

    def send_ask(dx, dy, dc):
        other = peer(dx, dy, dc)
        pltpu.make_async_remote_copy(
            src_ref=ask.at[other], dst_ref=asked_v.at[code(dx, dy, dc)], send_sem=q_send, recv_sem=q_recv,
            device_id={"pt": other}, device_id_type=MESH,
        ).start()

    each_offset(send_ask)
    asked_v[N_PT - 1] = ask[me]
    spread = [
        pltpu.make_async_remote_copy(
            src_ref=field.at[pl.ds(level * OWN, OWN)], dst_ref=field.at[pl.ds(level * OWN, OWN)],
            send_sem=z_send.at[d - 1], recv_sem=z_recv.at[d - 1], device_id=above(d), device_id_type=MESH,
        )
        for d in range(1, N_VAR)
    ]
    for copy in spread:
        copy.start()

    slip_copy.wait()
    lane16 = lax.broadcasted_iota(jnp.int32, (16, LANES), 1) // 32

    def turn(g, carry):
        for n in range(BLOCKS):
            piece = slip[pl.ds(4 * g, 4), :, LANES * n : LANES * (n + 1)].reshape(LANES, LANES)
            flipped = jnp.transpose(piece)
            for half in range(2):
                rows = [flipped[16 * (4 * half + q) : 16 * (4 * half + q) + 16, :] for q in range(4)]
                for v in range(4):
                    mixed = rows[v]
                    for q in range(4):
                        if q != v:
                            mixed = jnp.where(lane16 == q, pltpu.roll(rows[q], 32 * ((q - v) % 4), 1), mixed)
                    xmat[
                        pl.ds(pl.multiple_of((4 * g + v) * 16, 16), 16),
                        256 * (BLOCKS - 1 - n) + LANES * half : 256 * (BLOCKS - 1 - n) + LANES * (half + 1),
                    ] = mixed
        return carry

    lax.fori_loop(0, 4, turn, 0)

    everyone = pltpu.make_async_remote_copy(
        src_ref=ask.at[pl.ds(0, N_PT - 1)], dst_ref=asked_v.at[pl.ds(0, N_PT - 1)], send_sem=q_send, recv_sem=q_recv,
        device_id=sibling, device_id_type=MESH,
    )
    everyone.wait_recv()
    to_scalar = pltpu.make_async_copy(asked_v, asked, ask_sem)
    to_scalar.start()
    for d in range(1, N_VAR):
        source = lax.rem(level + (N_VAR - d), N_VAR)
        pltpu.make_async_remote_copy(
            src_ref=field.at[pl.ds(level * OWN, OWN)], dst_ref=field.at[pl.ds(source * OWN, OWN)],
            send_sem=z_send.at[d - 1], recv_sem=z_recv.at[d - 1], device_id=above(d), device_id_type=MESH,
        ).wait_recv()

    for p in range(HELD):
        field32[p] = field[p].astype(F32)
    to_scalar.wait()

    def answer(where, half):
        rows = [field32[asked[where, 0, slot], 8 * half : 8 * half + 8, :] for slot in range(2)]
        return jnp.concatenate(rows, axis=0).astype(BF16)

    inbox = [inbox_0, inbox_1]
    for half in range(2):

        def serve(dx, dy, dc):
            place = code(dx, dy, dc)
            outbox[half, place] = answer(code(lax.rem(4 - dx, 4), lax.rem(4 - dy, 4), dc), half)
            pltpu.make_async_remote_copy(
                src_ref=outbox.at[half, place], dst_ref=inbox[half].at[place],
                send_sem=g_send.at[half], recv_sem=g_recv.at[half], device_id={"pt": peer(dx, dy, dc)},
                device_id_type=MESH,
            ).start()

        each_offset(serve)
    for half in range(2):
        inbox[half][N_PT - 1] = answer(N_PT - 1, half)
        inbox[half][N_PT] = jnp.zeros((16, LANES), BF16)
    boxes = [
        pltpu.make_async_remote_copy(
            src_ref=outbox.at[half], dst_ref=inbox[half].at[pl.ds(0, N_PT - 1)],
            send_sem=g_send.at[half], recv_sem=g_recv.at[half], device_id=sibling, device_id_type=MESH,
        )
        for half in range(2)
    ]
    everyone.wait_send()
    for copy in spread:
        copy.wait_send()

    lane32 = lax.broadcasted_iota(jnp.int32, (HELD, LANES), 1)
    wide = lax.broadcasted_iota(jnp.int32, (VARS, 2 * LANES), 1) % LANES
    group8 = lax.broadcasted_iota(jnp.int32, (8, LANES), 1) // 32

    def delay(half, before):
        for r in range(HELD):
            both = inbox[half][pick_s[r]].astype(F32)
            gathered[8 * r : 8 * r + 8, :] = jnp.where(second_s[r] == 1, both[8:], both[:8])
        last = []
        for h in range(2):
            previous = before[h]
            for m in range(4 * half, 4 * half + 4):
                here = gathered[pl.ds(4 * h + m % 4, HELD, stride=8), :].astype(BF16)
                for c in range(BLOCKS):
                    if c == 0:
                        delayed = here
                    else:
                        delayed = jnp.where(
                            lane32 >= 16 * c, pltpu.roll(here, 16 * c, 1), pltpu.roll(previous, 16 * c, 1)
                        )
                    gmat[256 * m + 32 * c : 256 * m + 32 * c + 32, LANES * h : LANES * (h + 1)] = delayed
                previous = here
            last.append(previous)
        return last

    def product(m, first, last):
        start = 256 * (BLOCKS - 1 - m + first)
        return jnp.dot(
            xmat[:, start : start + 256 * (last - first)], gmat[256 * first : 256 * last, :], preferred_element_type=F32
        )

    def finish(m, spill):
        total = spill
        spill = jnp.zeros((VARS, 2 * LANES), F32)
        for f in range(16):
            rows = [zmat[m, h, pl.ds(f, VARS, stride=16), :] for h in range(2)]
            if f == 0:
                total = total + jnp.concatenate(rows, axis=1)
            else:
                rolled = jnp.concatenate([pltpu.roll(rows[h], f, 1) for h in range(2)], axis=1)
                kept = jnp.where(wide >= f, rolled, 0.0)
                total = total + kept
                spill = spill + (rolled - kept)
        quarters = [total[8 * (q // 2) : 8 * (q // 2) + 8, LANES * (q % 2) : LANES * (q % 2) + LANES] for q in range(4)]
        for t in range(4):
            mixed = quarters[t]
            for q in range(4):
                if q != t:
                    mixed = jnp.where(group8 == q, pltpu.roll(quarters[q], 32 * ((q - t) % 4), 1), mixed)
            part[4 * m + t] = mixed
        return spill

    def hand_out(half):
        def step(i, carry):
            other = (N_PT // 2) * half + lax.rem(me + i, N_PT // 2)
            place = (
                8 * lax.rem(lax.div(other, 8) + 4 - at_x, 4)
                + 2 * lax.rem(lax.rem(lax.div(other, 2), 4) + 4 - at_y, 4)
                + lax.rem(lax.rem(other, 2) + at_c, 2)
            )

            @pl.when(other != me)
            def _():
                pltpu.make_async_remote_copy(
                    src_ref=part.at[other], dst_ref=landed.at[lax.rem(place + N_PT - 1, N_PT)],
                    send_sem=y_send, recv_sem=y_recv, device_id={"pt": other}, device_id_type=MESH,
                ).start()

            return carry

        lax.fori_loop(0, N_PT // 2, step, 0)

    boxes[0].wait_recv()
    last = delay(0, [jnp.zeros((HELD, LANES), BF16)] * 2)
    spill = jnp.zeros((VARS, 2 * LANES), F32)
    for m in range(BLOCKS):
        whole = product(m, 0, min(m + 1, 4))
        zmat[m, 0] = whole[:, :LANES]
        zmat[m, 1] = whole[:, LANES:]
        if m < 4:
            spill = finish(m, spill)
        if m == 3:
            hand_out(0)

    boxes[1].wait_recv()
    delay(1, last)
    for m in range(4, BLOCKS):
        rest = product(m, 4, m + 1)
        zmat[m, 0] += rest[:, :LANES]
        zmat[m, 1] += rest[:, LANES:]
        spill = finish(m, spill)
    hand_out(1)
    mine = part[me]
    parts = pltpu.make_async_remote_copy(
        src_ref=part.at[pl.ds(0, N_PT - 1)], dst_ref=landed, send_sem=y_send, recv_sem=y_recv,
        device_id=sibling, device_id_type=MESH,
    )
    for copy in boxes:
        copy.wait_send()
    parts.wait_recv()
    mine = mine + jnp.sum(landed[...], axis=0)
    for q in range(4):
        out_ref[8 * (q // 2) : 8 * (q // 2) + 8, q % 2, :] = mine[:, 32 * q : 32 * q + 32]
    parts.wait_send()


def on_device(green_tensor, moment, slip_rate, owner_shard, point_slot, live_counts):
    hbm = pl.BlockSpec(memory_space=pl.ANY)
    vmem = pl.BlockSpec(memory_space=pltpu.VMEM)
    dma = pltpu.SemaphoreType.DMA
    length = slip_rate.shape[2]
    return pl.pallas_call(
        kernel,
        out_shape=jax.ShapeDtypeStruct((VARS, 2, 32), F32),
        in_specs=[hbm] * 5 + [pl.BlockSpec(memory_space=pltpu.SMEM)],
        out_specs=vmem,
        scratch_shapes=[
            pltpu.VMEM((VARS, HELD, length), BF16),
            pltpu.VMEM((96, length), BF16),
            pltpu.VMEM(moment.shape, BF16),
            pltpu.SMEM((1, HELD), jnp.int32),
            pltpu.SMEM((HELD,), jnp.int32),
            pltpu.VMEM((LANES, LANES), F32),
            pltpu.VMEM((HELD, 16, LANES), BF16),
            pltpu.VMEM((N_PT, 1, LANES), jnp.int32),
            pltpu.VMEM((N_PT, 1, LANES), jnp.int32),
            pltpu.SMEM((N_PT, 1, LANES), jnp.int32),
            pltpu.SMEM((HELD,), jnp.int32),
            pltpu.SMEM((HELD,), jnp.int32),
            pltpu.VMEM((HELD, 16, LANES), F32),
            pltpu.VMEM((2, N_PT - 1, 16, LANES), BF16),
            pltpu.VMEM((N_PT + 1, 16, LANES), BF16),
            pltpu.VMEM((N_PT + 1, 16, LANES), BF16),
            pltpu.VMEM((HELD * 8, LANES), F32),
            pltpu.VMEM((VARS * 16, 256 * BLOCKS), BF16),
            pltpu.VMEM((256 * BLOCKS, 2 * LANES), BF16),
            pltpu.VMEM((BLOCKS, 2, VARS * 16, LANES), F32),
            pltpu.VMEM((N_PT, 8, LANES), F32),
            pltpu.VMEM((N_PT - 1, 8, LANES), F32),
            dma, dma, dma((3,)), dma, dma((N_VAR - 1,)), dma((N_VAR - 1,)), dma, dma, dma((2,)), dma((2,)), dma, dma,
        ],
        compiler_params=pltpu.CompilerParams(
            collective_id=0, has_side_effects=True, vmem_limit_bytes=60 * 1024 * 1024
        ),
        name="synthesis",
    )(slip_rate, green_tensor.reshape(96, length), moment, owner_shard.reshape(1, HELD), point_slot, live_counts)


def solution(mesh):
    in_specs = (
        P(None, None, ("pt", "var"), None),
        P(None, ("pt", "var")),
        P("var", "pt", None),
        P("pt", None),
        P("pt"),
        P("pt"),
    )
    out_specs = P("var", None, "pt")
    return jax.shard_map(on_device, mesh=mesh, in_specs=in_specs, out_specs=out_specs, check_vma=False)
```

```python
import functools

import jax
import jax.numpy as jnp
from jax import lax
from jax.experimental import pallas as pl
from jax.experimental.pallas import tpu as pltpu
from jax.sharding import PartitionSpec as P

F32 = jnp.float32
BF16 = jnp.bfloat16
LANES = 128
N_PT = 32
N_VAR = 4
HELD = 32
OWN = 8
BLOCKS = 8
VARS = 16
MESH = pl.DeviceIdType.MESH


def offsets():
    every = [(dx, dy, dc) for dx in range(4) for dy in range(4) for dc in range(2)]
    return sorted(every[1:], key=lambda d: -(min(d[0], 4 - d[0]) + min(d[1], 4 - d[1])))


def each_offset(body, near_first=False):
    for dx, dy, dc in reversed(offsets()) if near_first else offsets():
        body(dx, dy, dc)


def code(dx, dy, dc):
    return (8 * dx + 2 * dy + dc + N_PT - 1) % N_PT


def rank_of(level):
    return jnp.where(level == 2, 3, jnp.where(level == 3, 2, level))


def request_table(owner_ref, slot_ref):
    row = lax.broadcasted_iota(jnp.int32, (N_PT, LANES), 0)
    lane = lax.broadcasted_iota(jnp.int32, (N_PT, LANES), 1)
    table = jnp.zeros((N_PT, LANES), jnp.int32)
    count = jnp.zeros((N_PT, LANES), jnp.int32)
    for r in range(HELD):
        hit = row == owner_ref[0, r]
        table = jnp.where(hit & (lane == count), slot_ref[r], table)
        count = count + hit.astype(jnp.int32)
    return table


def kernel(
    slip_hbm, green_hbm, moment_hbm, owner_hbm, slot_hbm, live_ref, out_ref,
    slip, green, moment, owner_ref, slot_ref, fold, field, ask, asked_v, asked, pick_s, second_s, field32, outbox, inbox_0, inbox_1,
    gathered, xmat, gmat, zmat, part, landed,
    slip_sem, green_sem, small_sem, ask_sem, z_go, z_send, z_recv, q_send, q_recv, g_send, g_recv, y_send, y_recv,
):
    me = lax.axis_index("pt")
    level = lax.axis_index("var")
    at_x, at_y, at_c = lax.div(me, 8), lax.rem(lax.div(me, 2), 4), lax.rem(me, 2)

    xs = [lax.rem(at_x + d, 4) for d in range(4)]
    ys = [lax.rem(at_y + d, 4) for d in range(4)]
    cs = [at_c, 1 - at_c]

    def peer(dx, dy, dc):
        return 8 * xs[dx] + 2 * ys[dy] + cs[dc]

    def above(d):
        return {"var": lax.rem(level + d, N_VAR)}

    sibling = {"pt": peer(0, 0, 1)}

    slip_copy = pltpu.make_async_copy(slip_hbm, slip, slip_sem)
    green_copy = pltpu.make_async_copy(green_hbm, green, green_sem)
    small = [
        pltpu.make_async_copy(source, here, small_sem.at[i])
        for i, (source, here) in enumerate(
            [(owner_hbm, owner_ref), (slot_hbm, slot_ref), (moment_hbm, moment)]
        )
    ]
    for one in small:
        one.start()
    green_copy.start()
    slip_copy.start()

    barrier = pltpu.get_barrier_semaphore()

    def greet(dx, dy, dc):
        pl.semaphore_signal(barrier, inc=1, device_id={"pt": peer(dx, dy, dc)}, device_id_type=MESH)

    each_offset(greet)
    rank = rank_of(level)
    first = [rank < rank_of(lax.rem(level + d, N_VAR)) for d in range(N_VAR)]
    for d in range(1, N_VAR):

        @pl.when(first[d])
        def _():
            pl.semaphore_signal(barrier, inc=1, device_id=above(d), device_id_type=MESH)

    for one in small:
        one.wait()
    table = request_table(owner_ref, slot_ref)
    for o in range(N_PT):
        ask[o] = table[o : o + 1, :]
    seen = jnp.int32(0)
    for r in range(HELD):
        owner = owner_ref[0, r]
        bit = jnp.left_shift(jnp.int32(1), owner)
        second = jnp.where((seen & bit) != 0, 1, 0)
        seen = seen | bit
        place = (
            8 * lax.rem(at_x + 4 - lax.div(owner, 8), 4)
            + 2 * lax.rem(at_y + 4 - lax.rem(lax.div(owner, 2), 4), 4)
            + lax.rem(at_c + lax.rem(owner, 2), 2)
        )
        place = lax.rem(place + N_PT - 1, N_PT)
        pick_s[r] = jnp.where(r < live_ref[0], place, N_PT)
        second_s[r] = second

    green_copy.wait()
    tall = jnp.transpose(moment[...].astype(F32))
    tall = jnp.concatenate([tall, tall], axis=0)
    for m in range(BLOCKS):
        total = jnp.zeros((2 * OWN, LANES), F32)
        for c in range(6):
            total = total + tall[:, c : c + 1] * green[16 * c : 16 * c + 16, LANES * m : LANES * (m + 1)].astype(F32)
        for h in range(2):
            row = OWN * (8 * (m // 4) + 4 * h + m % 4)
            fold[row : row + OWN, :] = total[OWN * h : OWN * h + OWN]
    for p in range(OWN):
        one = jnp.concatenate([fold[pl.ds(p, 8, stride=OWN), :], fold[pl.ds(64 + p, 8, stride=OWN), :]], axis=0)
        field[level * OWN + p] = one.astype(BF16)

    pl.semaphore_wait(barrier, N_PT - 1 + rank)
    for d in range(1, N_VAR):

        @pl.when(jnp.logical_not(first[d]))
        def _():
            pl.semaphore_signal(z_go.at[N_VAR - 1 - d], inc=1, device_id=above(d), device_id_type=MESH)

    def send_ask(dx, dy, dc):
        other = peer(dx, dy, dc)
        pltpu.make_async_remote_copy(
            src_ref=ask.at[other], dst_ref=asked_v.at[code(dx, dy, dc)], send_sem=q_send, recv_sem=q_recv,
            device_id={"pt": other}, device_id_type=MESH,
        ).start()

    each_offset(send_ask)
    asked_v[N_PT - 1] = ask[me]
    spread = [
        pltpu.make_async_remote_copy(
            src_ref=field.at[pl.ds(level * OWN, OWN)], dst_ref=field.at[pl.ds(level * OWN, OWN)],
            send_sem=z_send.at[d - 1], recv_sem=z_recv.at[d - 1], device_id=above(d), device_id_type=MESH,
        )
        for d in range(1, N_VAR)
    ]
    for d in range(1, N_VAR):

        @pl.when(jnp.logical_not(first[d]))
        def _():
            spread[d - 1].start()

    slip_copy.wait()
    lane16 = lax.broadcasted_iota(jnp.int32, (16, LANES), 1) // 32

    def turn(g, carry):
        for n in range(BLOCKS):
            piece = slip[pl.ds(4 * g, 4), :, LANES * n : LANES * (n + 1)].reshape(LANES, LANES)
            flipped = jnp.transpose(piece)
            for half in range(2):
                rows = [flipped[16 * (4 * half + q) : 16 * (4 * half + q) + 16, :] for q in range(4)]
                for v in range(4):
                    mixed = rows[v]
                    for q in range(4):
                        if q != v:
                            mixed = jnp.where(lane16 == q, pltpu.roll(rows[q], 32 * ((q - v) % 4), 1), mixed)
                    xmat[
                        pl.ds(pl.multiple_of((4 * g + v) * 16, 16), 16),
                        256 * (BLOCKS - 1 - n) + LANES * half : 256 * (BLOCKS - 1 - n) + LANES * (half + 1),
                    ] = mixed
        return carry

    lax.fori_loop(0, 4, turn, 0)

    for d in range(1, N_VAR):

        @pl.when(first[d])
        def _():
            pl.semaphore_wait(z_go.at[d - 1], 1)
            spread[d - 1].start()

    everyone = pltpu.make_async_remote_copy(
        src_ref=ask.at[pl.ds(0, N_PT - 1)], dst_ref=asked_v.at[pl.ds(0, N_PT - 1)], send_sem=q_send, recv_sem=q_recv,
        device_id=sibling, device_id_type=MESH,
    )
    everyone.wait_recv()
    to_scalar = pltpu.make_async_copy(asked_v, asked, ask_sem)
    to_scalar.start()
    for d in range(1, N_VAR):
        source = lax.rem(level + (N_VAR - d), N_VAR)
        pltpu.make_async_remote_copy(
            src_ref=field.at[pl.ds(level * OWN, OWN)], dst_ref=field.at[pl.ds(source * OWN, OWN)],
            send_sem=z_send.at[d - 1], recv_sem=z_recv.at[d - 1], device_id=above(d), device_id_type=MESH,
        ).wait_recv()

    for p in range(HELD):
        field32[p] = field[p].astype(F32)
    to_scalar.wait()

    def answer(where, half):
        rows = [field32[asked[where, 0, slot], 8 * half : 8 * half + 8, :] for slot in range(2)]
        return jnp.concatenate(rows, axis=0).astype(BF16)

    inbox = [inbox_0, inbox_1]
    for half in range(2):

        def serve(dx, dy, dc):
            place = code(dx, dy, dc)
            outbox[half, place] = answer(code(-dx % 4, -dy % 4, dc), half)
            pltpu.make_async_remote_copy(
                src_ref=outbox.at[half, place], dst_ref=inbox[half].at[place],
                send_sem=g_send.at[half], recv_sem=g_recv.at[half], device_id={"pt": peer(dx, dy, dc)},
                device_id_type=MESH,
            ).start()

        each_offset(serve)
    for half in range(2):
        inbox[half][N_PT - 1] = answer(N_PT - 1, half)
        inbox[half][N_PT] = jnp.zeros((16, LANES), BF16)
    boxes = [
        pltpu.make_async_remote_copy(
            src_ref=outbox.at[half], dst_ref=inbox[half].at[pl.ds(0, N_PT - 1)],
            send_sem=g_send.at[half], recv_sem=g_recv.at[half], device_id=sibling, device_id_type=MESH,
        )
        for half in range(2)
    ]
    everyone.wait_send()
    for copy in spread:
        copy.wait_send()

    lane32 = lax.broadcasted_iota(jnp.int32, (HELD, LANES), 1)
    wide = lax.broadcasted_iota(jnp.int32, (VARS, 2 * LANES), 1) % LANES
    group8 = lax.broadcasted_iota(jnp.int32, (8, LANES), 1) // 32

    def delay(half, before):
        for r in range(HELD):
            both = inbox[half][pick_s[r]].astype(F32)
            gathered[8 * r : 8 * r + 8, :] = jnp.where(second_s[r] == 1, both[8:], both[:8])
        last = []
        for h in range(2):
            previous = before[h]
            for m in range(4 * half, 4 * half + 4):
                here = gathered[pl.ds(4 * h + m % 4, HELD, stride=8), :].astype(BF16)
                for c in range(BLOCKS):
                    if c == 0:
                        delayed = here
                    else:
                        delayed = jnp.where(
                            lane32 >= 16 * c, pltpu.roll(here, 16 * c, 1), pltpu.roll(previous, 16 * c, 1)
                        )
                    gmat[256 * m + 32 * c : 256 * m + 32 * c + 32, LANES * h : LANES * (h + 1)] = delayed
                previous = here
            last.append(previous)
        return last

    def product(m, first, last):
        start = 256 * (BLOCKS - 1 - m + first)
        return jnp.dot(
            xmat[:, start : start + 256 * (last - first)], gmat[256 * first : 256 * last, :], preferred_element_type=F32
        )

    def finish(m, spill):
        total = spill
        spill = jnp.zeros((VARS, 2 * LANES), F32)
        for f in range(16):
            rows = [zmat[m, h, pl.ds(f, VARS, stride=16), :] for h in range(2)]
            if f == 0:
                total = total + jnp.concatenate(rows, axis=1)
            else:
                rolled = jnp.concatenate([pltpu.roll(rows[h], f, 1) for h in range(2)], axis=1)
                kept = jnp.where(wide >= f, rolled, 0.0)
                total = total + kept
                spill = spill + (rolled - kept)
        quarters = [total[8 * (q // 2) : 8 * (q // 2) + 8, LANES * (q % 2) : LANES * (q % 2) + LANES] for q in range(4)]
        for t in range(4):
            mixed = quarters[t]
            for q in range(4):
                if q != t:
                    mixed = jnp.where(group8 == q, pltpu.roll(quarters[q], 32 * ((q - t) % 4), 1), mixed)
            part[4 * m + t] = mixed
        return spill

    def hand_out(half):
        def step(i, carry):
            other = (N_PT // 2) * half + lax.rem(me + i, N_PT // 2)
            place = (
                8 * lax.rem(lax.div(other, 8) + 4 - at_x, 4)
                + 2 * lax.rem(lax.rem(lax.div(other, 2), 4) + 4 - at_y, 4)
                + lax.rem(lax.rem(other, 2) + at_c, 2)
            )

            @pl.when(other != me)
            def _():
                pltpu.make_async_remote_copy(
                    src_ref=part.at[other], dst_ref=landed.at[lax.rem(place + N_PT - 1, N_PT)],
                    send_sem=y_send, recv_sem=y_recv, device_id={"pt": other}, device_id_type=MESH,
                ).start()

            return carry

        lax.fori_loop(0, N_PT // 2, step, 0)

    boxes[0].wait_recv()
    last = delay(0, [jnp.zeros((HELD, LANES), BF16)] * 2)
    spill = jnp.zeros((VARS, 2 * LANES), F32)
    for m in range(BLOCKS):
        whole = product(m, 0, min(m + 1, 4))
        zmat[m, 0] = whole[:, :LANES]
        zmat[m, 1] = whole[:, LANES:]
        if m < 4:
            spill = finish(m, spill)
        if m == 3:
            hand_out(0)

    boxes[1].wait_recv()
    delay(1, last)
    for m in range(4, BLOCKS):
        rest = product(m, 4, m + 1)
        zmat[m, 0] += rest[:, :LANES]
        zmat[m, 1] += rest[:, LANES:]
        spill = finish(m, spill)
    hand_out(1)
    mine = part[me]
    parts = pltpu.make_async_remote_copy(
        src_ref=part.at[pl.ds(0, N_PT - 1)], dst_ref=landed, send_sem=y_send, recv_sem=y_recv,
        device_id=sibling, device_id_type=MESH,
    )
    for copy in boxes:
        copy.wait_send()
    parts.wait_recv()
    mine = mine + jnp.sum(landed[...], axis=0)
    for q in range(4):
        out_ref[8 * (q // 2) : 8 * (q // 2) + 8, q % 2, :] = mine[:, 32 * q : 32 * q + 32]
    parts.wait_send()


def on_device(green_tensor, moment, slip_rate, owner_shard, point_slot, live_counts):
    hbm = pl.BlockSpec(memory_space=pl.ANY)
    vmem = pl.BlockSpec(memory_space=pltpu.VMEM)
    dma = pltpu.SemaphoreType.DMA
    length = slip_rate.shape[2]
    return pl.pallas_call(
        kernel,
        out_shape=jax.ShapeDtypeStruct((VARS, 2, 32), F32),
        in_specs=[hbm] * 5 + [pl.BlockSpec(memory_space=pltpu.SMEM)],
        out_specs=vmem,
        scratch_shapes=[
            pltpu.VMEM((VARS, HELD, length), BF16),
            pltpu.VMEM((96, length), BF16),
            pltpu.VMEM(moment.shape, BF16),
            pltpu.SMEM((1, HELD), jnp.int32),
            pltpu.SMEM((HELD,), jnp.int32),
            pltpu.VMEM((LANES, LANES), F32),
            pltpu.VMEM((HELD, 16, LANES), BF16),
            pltpu.VMEM((N_PT, 1, LANES), jnp.int32),
            pltpu.VMEM((N_PT, 1, LANES), jnp.int32),
            pltpu.SMEM((N_PT, 1, LANES), jnp.int32),
            pltpu.SMEM((HELD,), jnp.int32),
            pltpu.SMEM((HELD,), jnp.int32),
            pltpu.VMEM((HELD, 16, LANES), F32),
            pltpu.VMEM((2, N_PT - 1, 16, LANES), BF16),
            pltpu.VMEM((N_PT + 1, 16, LANES), BF16),
            pltpu.VMEM((N_PT + 1, 16, LANES), BF16),
            pltpu.VMEM((HELD * 8, LANES), F32),
            pltpu.VMEM((VARS * 16, 256 * BLOCKS), BF16),
            pltpu.VMEM((256 * BLOCKS, 2 * LANES), BF16),
            pltpu.VMEM((BLOCKS, 2, VARS * 16, LANES), F32),
            pltpu.VMEM((N_PT, 8, LANES), F32),
            pltpu.VMEM((N_PT - 1, 8, LANES), F32),
            dma, dma, dma((3,)), dma, pltpu.SemaphoreType.REGULAR((N_VAR - 1,)), dma((N_VAR - 1,)), dma((N_VAR - 1,)), dma, dma, dma((2,)), dma((2,)), dma, dma,
        ],
        compiler_params=pltpu.CompilerParams(
            collective_id=0, has_side_effects=True, vmem_limit_bytes=55168 * 1024
        ),
        name="synthesis",
    )(slip_rate, green_tensor.reshape(96, length), moment, owner_shard.reshape(1, HELD), point_slot, live_counts)


def solution(mesh):
    in_specs = (
        P(None, None, ("pt", "var"), None),
        P(None, ("pt", "var")),
        P("var", "pt", None),
        P("pt", None),
        P("pt"),
        P("pt"),
    )
    out_specs = P("var", None, "pt")
    return jax.shard_map(on_device, mesh=mesh, in_specs=in_specs, out_specs=out_specs, check_vma=False)
```

```python
import functools

import jax
import jax.numpy as jnp
from jax import lax
from jax.experimental import pallas as pl
from jax.experimental.pallas import tpu as pltpu
from jax.sharding import PartitionSpec as P

F32 = jnp.float32
BF16 = jnp.bfloat16
LANES = 128
N_PT = 32
N_VAR = 4
HELD = 32
OWN = 8
BLOCKS = 8
VARS = 16
MESH = pl.DeviceIdType.MESH


def offsets():
    every = [(dx, dy, dc) for dx in range(4) for dy in range(4) for dc in range(2)]
    return sorted(every[1:], key=lambda d: -(min(d[0], 4 - d[0]) + min(d[1], 4 - d[1])))


def each_offset(body, near_first=False):
    for dx, dy, dc in reversed(offsets()) if near_first else offsets():
        body(dx, dy, dc)


def code(dx, dy, dc):
    return (8 * dx + 2 * dy + dc + N_PT - 1) % N_PT


def rank_of(level):
    return jnp.where(level == 2, 3, jnp.where(level == 3, 2, level))


def request_table(owner_ref, slot_ref):
    row = lax.broadcasted_iota(jnp.int32, (N_PT, LANES), 0)
    lane = lax.broadcasted_iota(jnp.int32, (N_PT, LANES), 1)
    table = jnp.zeros((N_PT, LANES), jnp.int32)
    count = jnp.zeros((N_PT, LANES), jnp.int32)
    for r in range(HELD):
        hit = row == owner_ref[0, r]
        table = jnp.where(hit & (lane == count), slot_ref[r], table)
        count = count + hit.astype(jnp.int32)
    return table


def kernel(
    slip_hbm, green_hbm, moment_hbm, owner_hbm, slot_hbm, live_ref, out_ref,
    slip, green, moment, owner_ref, slot_ref, fold, field, ask, asked_v, asked, pick_s, second_s, field32, outbox, inbox_0, inbox_1,
    gathered, xmat, gmat, zmat, part, landed,
    slip_sem, green_sem, small_sem, ask_sem, z_go, z_send, z_recv, q_send, q_recv, g_send, g_recv, y_send, y_recv,
):
    me = lax.axis_index("pt")
    level = lax.axis_index("var")
    at_x, at_y, at_c = lax.div(me, 8), lax.rem(lax.div(me, 2), 4), lax.rem(me, 2)

    xs = [lax.rem(at_x + d, 4) for d in range(4)]
    ys = [lax.rem(at_y + d, 4) for d in range(4)]
    cs = [at_c, 1 - at_c]

    def peer(dx, dy, dc):
        return 8 * xs[dx] + 2 * ys[dy] + cs[dc]

    def above(d):
        return {"var": lax.rem(level + d, N_VAR)}

    sibling = {"pt": peer(0, 0, 1)}

    slip_copy = pltpu.make_async_copy(slip_hbm, slip, slip_sem)
    green_copy = pltpu.make_async_copy(green_hbm, green, green_sem)
    small = [
        pltpu.make_async_copy(source, here, small_sem.at[i])
        for i, (source, here) in enumerate(
            [(owner_hbm, owner_ref), (slot_hbm, slot_ref), (moment_hbm, moment)]
        )
    ]
    for one in small:
        one.start()
    green_copy.start()
    slip_copy.start()

    barrier = pltpu.get_barrier_semaphore()

    def greet(dx, dy, dc):
        pl.semaphore_signal(barrier, inc=1, device_id={"pt": peer(dx, dy, dc)}, device_id_type=MESH)

    each_offset(greet)
    rank = rank_of(level)
    first = [rank < rank_of(lax.rem(level + d, N_VAR)) for d in range(N_VAR)]
    for d in range(1, N_VAR):

        @pl.when(first[d])
        def _():
            pl.semaphore_signal(barrier, inc=1, device_id=above(d), device_id_type=MESH)

    for one in small:
        one.wait()
    table = request_table(owner_ref, slot_ref)
    for o in range(N_PT):
        ask[o] = table[o : o + 1, :]
    seen = jnp.int32(0)
    for r in range(HELD):
        owner = owner_ref[0, r]
        bit = jnp.left_shift(jnp.int32(1), owner)
        second = jnp.where((seen & bit) != 0, 1, 0)
        seen = seen | bit
        place = (
            8 * lax.rem(at_x + 4 - lax.div(owner, 8), 4)
            + 2 * lax.rem(at_y + 4 - lax.rem(lax.div(owner, 2), 4), 4)
            + lax.rem(at_c + lax.rem(owner, 2), 2)
        )
        place = lax.rem(place + N_PT - 1, N_PT)
        pick_s[r] = jnp.where(r < live_ref[0], place, N_PT)
        second_s[r] = second

    green_copy.wait()
    tall = jnp.transpose(moment[...].astype(F32))
    tall = jnp.concatenate([tall, tall], axis=0)
    for m in range(BLOCKS):
        total = jnp.zeros((2 * OWN, LANES), F32)
        for c in range(6):
            total = total + tall[:, c : c + 1] * green[16 * c : 16 * c + 16, LANES * m : LANES * (m + 1)].astype(F32)
        for h in range(2):
            row = OWN * (8 * (m // 4) + 4 * h + m % 4)
            fold[row : row + OWN, :] = total[OWN * h : OWN * h + OWN]
    for p in range(OWN):
        one = jnp.concatenate([fold[pl.ds(p, 8, stride=OWN), :], fold[pl.ds(64 + p, 8, stride=OWN), :]], axis=0)
        field[level * OWN + p] = one.astype(BF16)

    pl.semaphore_wait(barrier, N_PT - 1 + rank)
    for d in range(1, N_VAR):

        @pl.when(jnp.logical_not(first[d]))
        def _():
            pl.semaphore_signal(z_go.at[N_VAR - 1 - d], inc=1, device_id=above(d), device_id_type=MESH)

    def send_ask(dx, dy, dc):
        other = peer(dx, dy, dc)
        pltpu.make_async_remote_copy(
            src_ref=ask.at[other], dst_ref=asked_v.at[code(dx, dy, dc)], send_sem=q_send, recv_sem=q_recv,
            device_id={"pt": other}, device_id_type=MESH,
        ).start()

    each_offset(send_ask)
    asked_v[N_PT - 1] = ask[me]
    spread = [
        pltpu.make_async_remote_copy(
            src_ref=field.at[pl.ds(level * OWN, OWN)], dst_ref=field.at[pl.ds(level * OWN, OWN)],
            send_sem=z_send.at[d - 1], recv_sem=z_recv.at[d - 1], device_id=above(d), device_id_type=MESH,
        )
        for d in range(1, N_VAR)
    ]
    for d in range(1, N_VAR):

        @pl.when(jnp.logical_not(first[d]))
        def _():
            spread[d - 1].start()

    slip_copy.wait()
    lane16 = lax.broadcasted_iota(jnp.int32, (16, LANES), 1) // 32

    def turn(g, carry):
        for n in range(BLOCKS):
            piece = slip[pl.ds(4 * g, 4), :, LANES * n : LANES * (n + 1)].reshape(LANES, LANES)
            flipped = jnp.transpose(piece)
            for half in range(2):
                rows = [flipped[16 * (4 * half + q) : 16 * (4 * half + q) + 16, :] for q in range(4)]
                for v in range(4):
                    mixed = rows[v]
                    for q in range(4):
                        if q != v:
                            mixed = jnp.where(lane16 == q, pltpu.roll(rows[q], 32 * ((q - v) % 4), 1), mixed)
                    xmat[
                        pl.ds(pl.multiple_of((4 * g + v) * 16, 16), 16),
                        256 * (BLOCKS - 1 - n) + LANES * half : 256 * (BLOCKS - 1 - n) + LANES * (half + 1),
                    ] = mixed
        return carry

    lax.fori_loop(0, 4, turn, 0)

    for d in range(1, N_VAR):

        @pl.when(first[d])
        def _():
            pl.semaphore_wait(z_go.at[d - 1], 1)
            spread[d - 1].start()

    everyone = pltpu.make_async_remote_copy(
        src_ref=ask.at[pl.ds(0, N_PT - 1)], dst_ref=asked_v.at[pl.ds(0, N_PT - 1)], send_sem=q_send, recv_sem=q_recv,
        device_id=sibling, device_id_type=MESH,
    )
    everyone.wait_recv()
    to_scalar = pltpu.make_async_copy(asked_v, asked, ask_sem)
    to_scalar.start()
    for d in range(1, N_VAR):
        source = lax.rem(level + (N_VAR - d), N_VAR)
        pltpu.make_async_remote_copy(
            src_ref=field.at[pl.ds(level * OWN, OWN)], dst_ref=field.at[pl.ds(source * OWN, OWN)],
            send_sem=z_send.at[d - 1], recv_sem=z_recv.at[d - 1], device_id=above(d), device_id_type=MESH,
        ).wait_recv()

    for p in range(HELD):
        field32[p] = field[p].astype(F32)
    to_scalar.wait()

    def answer(where, half):
        rows = [field32[asked[where, 0, slot], 8 * half : 8 * half + 8, :] for slot in range(2)]
        return jnp.concatenate(rows, axis=0).astype(BF16)

    inbox = [inbox_0, inbox_1]
    for half in range(2):

        def serve(dx, dy, dc):
            place = code(dx, dy, dc)
            outbox[half, place] = answer(code(-dx % 4, -dy % 4, dc), half)
            pltpu.make_async_remote_copy(
                src_ref=outbox.at[half, place], dst_ref=inbox[half].at[place],
                send_sem=g_send.at[half], recv_sem=g_recv.at[half], device_id={"pt": peer(dx, dy, dc)},
                device_id_type=MESH,
            ).start()

        each_offset(serve)
    for half in range(2):
        inbox[half][N_PT - 1] = answer(N_PT - 1, half)
        inbox[half][N_PT] = jnp.zeros((16, LANES), BF16)
    boxes = [
        pltpu.make_async_remote_copy(
            src_ref=outbox.at[half], dst_ref=inbox[half].at[pl.ds(0, N_PT - 1)],
            send_sem=g_send.at[half], recv_sem=g_recv.at[half], device_id=sibling, device_id_type=MESH,
        )
        for half in range(2)
    ]
    everyone.wait_send()
    for copy in spread:
        copy.wait_send()

    lane32 = lax.broadcasted_iota(jnp.int32, (HELD, LANES), 1)
    wide = lax.broadcasted_iota(jnp.int32, (VARS, 2 * LANES), 1) % LANES
    group8 = lax.broadcasted_iota(jnp.int32, (8, LANES), 1) // 32

    def delay(half, before):
        for r in range(HELD):
            both = inbox[half][pick_s[r]].astype(F32)
            gathered[8 * r : 8 * r + 8, :] = jnp.where(second_s[r] == 1, both[8:], both[:8])
        last = []
        for h in range(2):
            previous = before[h]
            for m in range(4 * half, 4 * half + 4):
                here = gathered[pl.ds(4 * h + m % 4, HELD, stride=8), :].astype(BF16)
                for c in range(BLOCKS):
                    if c == 0:
                        delayed = here
                    else:
                        delayed = jnp.where(
                            lane32 >= 16 * c, pltpu.roll(here, 16 * c, 1), pltpu.roll(previous, 16 * c, 1)
                        )
                    gmat[256 * m + 32 * c : 256 * m + 32 * c + 32, LANES * h : LANES * (h + 1)] = delayed
                previous = here
            last.append(previous)
        return last

    def product(m, first, last):
        start = 256 * (BLOCKS - 1 - m + first)
        return jnp.dot(
            xmat[:, start : start + 256 * (last - first)], gmat[256 * first : 256 * last, :], preferred_element_type=F32
        )

    def finish(m, spill):
        total = spill
        spill = jnp.zeros((VARS, 2 * LANES), F32)
        for f in range(16):
            rows = [zmat[m, h, pl.ds(f, VARS, stride=16), :] for h in range(2)]
            if f == 0:
                total = total + jnp.concatenate(rows, axis=1)
            else:
                rolled = jnp.concatenate([pltpu.roll(rows[h], f, 1) for h in range(2)], axis=1)
                kept = jnp.where(wide >= f, rolled, 0.0)
                total = total + kept
                spill = spill + (rolled - kept)
        quarters = [total[8 * (q // 2) : 8 * (q // 2) + 8, LANES * (q % 2) : LANES * (q % 2) + LANES] for q in range(4)]
        for t in range(4):
            mixed = quarters[t]
            for q in range(4):
                if q != t:
                    mixed = jnp.where(group8 == q, pltpu.roll(quarters[q], 32 * ((q - t) % 4), 1), mixed)
            part[4 * m + t] = mixed
        return spill

    def hand_out(half):
        def step(i, carry):
            other = (N_PT // 2) * half + lax.rem(me + i, N_PT // 2)
            place = (
                8 * lax.rem(lax.div(other, 8) + 4 - at_x, 4)
                + 2 * lax.rem(lax.rem(lax.div(other, 2), 4) + 4 - at_y, 4)
                + lax.rem(lax.rem(other, 2) + at_c, 2)
            )

            @pl.when(other != me)
            def _():
                pltpu.make_async_remote_copy(
                    src_ref=part.at[other], dst_ref=landed.at[lax.rem(place + N_PT - 1, N_PT)],
                    send_sem=y_send, recv_sem=y_recv, device_id={"pt": other}, device_id_type=MESH,
                ).start()

            return carry

        lax.fori_loop(0, N_PT // 2, step, 0)

    boxes[0].wait_recv()
    last = delay(0, [jnp.zeros((HELD, LANES), BF16)] * 2)
    spill = jnp.zeros((VARS, 2 * LANES), F32)
    for m in range(BLOCKS):
        whole = product(m, 0, min(m + 1, 4))
        zmat[m, 0] = whole[:, :LANES]
        zmat[m, 1] = whole[:, LANES:]
        if m < 4:
            spill = finish(m, spill)
        if m == 3:
            hand_out(0)

    boxes[1].wait_recv()
    delay(1, last)
    for m in range(4, BLOCKS):
        rest = product(m, 4, m + 1)
        zmat[m, 0] += rest[:, :LANES]
        zmat[m, 1] += rest[:, LANES:]
        spill = finish(m, spill)
    hand_out(1)
    mine = part[me]
    parts = pltpu.make_async_remote_copy(
        src_ref=part.at[pl.ds(0, N_PT - 1)], dst_ref=landed, send_sem=y_send, recv_sem=y_recv,
        device_id=sibling, device_id_type=MESH,
    )
    for copy in boxes:
        copy.wait_send()
    parts.wait_recv()
    mine = mine + jnp.sum(landed[...], axis=0)
    for q in range(4):
        out_ref[8 * (q // 2) : 8 * (q // 2) + 8, q % 2, :] = mine[:, 32 * q : 32 * q + 32]
    parts.wait_send()


def on_device(green_tensor, moment, slip_rate, owner_shard, point_slot, live_counts):
    hbm = pl.BlockSpec(memory_space=pltpu.HBM)
    vmem = pl.BlockSpec(memory_space=pltpu.VMEM)
    dma = pltpu.SemaphoreType.DMA
    length = slip_rate.shape[2]
    in_hbm = [
        pltpu.with_memory_space_constraint(a, pltpu.HBM)
        for a in (slip_rate, green_tensor.reshape(96, length), moment, owner_shard.reshape(1, HELD), point_slot)
    ]
    return pl.pallas_call(
        kernel,
        out_shape=jax.ShapeDtypeStruct((VARS, 2, 32), F32),
        in_specs=[hbm] * 5 + [pl.BlockSpec(memory_space=pltpu.SMEM)],
        out_specs=vmem,
        scratch_shapes=[
            pltpu.VMEM((VARS, HELD, length), BF16),
            pltpu.VMEM((96, length), BF16),
            pltpu.VMEM(moment.shape, BF16),
            pltpu.SMEM((1, HELD), jnp.int32),
            pltpu.SMEM((HELD,), jnp.int32),
            pltpu.VMEM((LANES, LANES), F32),
            pltpu.VMEM((HELD, 16, LANES), BF16),
            pltpu.VMEM((N_PT, 1, LANES), jnp.int32),
            pltpu.VMEM((N_PT, 1, LANES), jnp.int32),
            pltpu.SMEM((N_PT, 1, LANES), jnp.int32),
            pltpu.SMEM((HELD,), jnp.int32),
            pltpu.SMEM((HELD,), jnp.int32),
            pltpu.VMEM((HELD, 16, LANES), F32),
            pltpu.VMEM((2, N_PT - 1, 16, LANES), BF16),
            pltpu.VMEM((N_PT + 1, 16, LANES), BF16),
            pltpu.VMEM((N_PT + 1, 16, LANES), BF16),
            pltpu.VMEM((HELD * 8, LANES), F32),
            pltpu.VMEM((VARS * 16, 256 * BLOCKS), BF16),
            pltpu.VMEM((256 * BLOCKS, 2 * LANES), BF16),
            pltpu.VMEM((BLOCKS, 2, VARS * 16, LANES), F32),
            pltpu.VMEM((N_PT, 8, LANES), F32),
            pltpu.VMEM((N_PT - 1, 8, LANES), F32),
            dma, dma, dma((3,)), dma, pltpu.SemaphoreType.REGULAR((N_VAR - 1,)), dma((N_VAR - 1,)), dma((N_VAR - 1,)), dma, dma, dma((2,)), dma((2,)), dma, dma,
        ],
        compiler_params=pltpu.CompilerParams(
            collective_id=0, has_side_effects=True, vmem_limit_bytes=32 * 1024 * 1024
        ),
        name="synthesis",
    )(*in_hbm, live_counts)


def solution(mesh):
    in_specs = (
        P(None, None, ("pt", "var"), None),
        P(None, ("pt", "var")),
        P("var", "pt", None),
        P("pt", None),
        P("pt"),
        P("pt"),
    )
    out_specs = P("var", None, "pt")
    return jax.shard_map(on_device, mesh=mesh, in_specs=in_specs, out_specs=out_specs, check_vma=False)
```

```python
import functools

import jax
import jax.numpy as jnp
from jax import lax
from jax.experimental import pallas as pl
from jax.experimental.pallas import tpu as pltpu
from jax.sharding import PartitionSpec as P

F32 = jnp.float32
BF16 = jnp.bfloat16
LANES = 128
N_PT = 32
N_VAR = 4
HELD = 32
OWN = 8
BLOCKS = 8
VARS = 16
MESH = pl.DeviceIdType.MESH


def offsets():
    every = [(dx, dy, dc) for dx in range(4) for dy in range(4) for dc in range(2)]
    return sorted(every[1:], key=lambda d: -(min(d[0], 4 - d[0]) + min(d[1], 4 - d[1])))


def each_offset(body, near_first=False):
    for dx, dy, dc in reversed(offsets()) if near_first else offsets():
        body(dx, dy, dc)


def code(dx, dy, dc):
    return (8 * dx + 2 * dy + dc + N_PT - 1) % N_PT


def rank_of(level):
    return jnp.where(level == 2, 3, jnp.where(level == 3, 2, level))


def request_table(owner_ref, slot_ref, at_x, at_y, at_c):
    row = lax.broadcasted_iota(jnp.int32, (N_PT, LANES), 0)
    lane = lax.broadcasted_iota(jnp.int32, (N_PT, LANES), 1)
    dx = (row // 8 + 4 - at_x) % 4
    dy = (row // 2 + 4 - at_y) % 4
    dc = (row + at_c) % 2
    free = 2 * ((8 * dx + 2 * dy + dc + N_PT - 1) % N_PT)
    table = jnp.zeros((N_PT, LANES), jnp.int32)
    for r in range(HELD):
        hit = row == owner_ref[0, r]
        table = jnp.where(hit & (lane == free), slot_ref[r], table)
        free = free + hit.astype(jnp.int32)
    return table


def kernel(
    slip_hbm, green_hbm, moment_hbm, owner_hbm, slot_hbm, live_ref, out_ref,
    slip, green, moment, owner_ref, slot_ref, fold, field, ask, asked_v, compact, asked, pick_s, second_s, outbox, inbox_0, inbox_1,
    gathered, xmat, gmat, zmat, part, landed,
    slip_sem, green_sem, small_sem, ask_sem, z_go, z_send, z_recv, q_send, q_recv, g_send, g_recv, y_send, y_recv,
):
    me = lax.axis_index("pt")
    level = lax.axis_index("var")
    at_x, at_y, at_c = lax.div(me, 8), lax.rem(lax.div(me, 2), 4), lax.rem(me, 2)

    xs = [lax.rem(at_x + d, 4) for d in range(4)]
    ys = [lax.rem(at_y + d, 4) for d in range(4)]
    cs = [at_c, 1 - at_c]

    def peer(dx, dy, dc):
        return 8 * xs[dx] + 2 * ys[dy] + cs[dc]

    def above(d):
        return {"var": lax.rem(level + d, N_VAR)}

    sibling = {"pt": peer(0, 0, 1)}

    slip_copy = pltpu.make_async_copy(slip_hbm, slip, slip_sem)
    green_copy = pltpu.make_async_copy(green_hbm, green, green_sem)
    small = [
        pltpu.make_async_copy(source, here, small_sem.at[i])
        for i, (source, here) in enumerate(
            [(owner_hbm, owner_ref), (slot_hbm, slot_ref), (moment_hbm, moment)]
        )
    ]
    for one in small:
        one.start()
    green_copy.start()
    slip_copy.start()

    barrier = pltpu.get_barrier_semaphore()

    def greet(dx, dy, dc):
        pl.semaphore_signal(barrier, inc=1, device_id={"pt": peer(dx, dy, dc)}, device_id_type=MESH)

    each_offset(greet)
    rank = rank_of(level)
    first = [rank < rank_of(lax.rem(level + d, N_VAR)) for d in range(N_VAR)]
    for d in range(1, N_VAR):

        @pl.when(first[d])
        def _():
            pl.semaphore_signal(barrier, inc=1, device_id=above(d), device_id_type=MESH)

    for one in small:
        one.wait()
    table = request_table(owner_ref, slot_ref, at_x, at_y, at_c)
    for o in range(N_PT):
        ask[o] = table[o : o + 1, :]
    seen = jnp.int32(0)
    for r in range(HELD):
        owner = owner_ref[0, r]
        bit = jnp.left_shift(jnp.int32(1), owner)
        second = jnp.where((seen & bit) != 0, 1, 0)
        seen = seen | bit
        place = (
            8 * lax.rem(at_x + 4 - lax.div(owner, 8), 4)
            + 2 * lax.rem(at_y + 4 - lax.rem(lax.div(owner, 2), 4), 4)
            + lax.rem(at_c + lax.rem(owner, 2), 2)
        )
        place = lax.rem(place + N_PT - 1, N_PT)
        pick_s[r] = jnp.where(r < live_ref[0], place, N_PT)
        second_s[r] = second

    green_copy.wait()
    tall = jnp.transpose(moment[...].astype(F32))
    tall = jnp.concatenate([tall, tall], axis=0)
    for m in range(BLOCKS):
        total = jnp.zeros((2 * OWN, LANES), F32)
        for c in range(6):
            total = total + tall[:, c : c + 1] * green[16 * c : 16 * c + 16, LANES * m : LANES * (m + 1)].astype(F32)
        for h in range(2):
            row = OWN * (8 * (m // 4) + 4 * h + m % 4)
            fold[row : row + OWN, :] = total[OWN * h : OWN * h + OWN]
    for p in range(OWN):
        one = jnp.concatenate([fold[pl.ds(p, 8, stride=OWN), :], fold[pl.ds(64 + p, 8, stride=OWN), :]], axis=0)
        field[level * OWN + p] = one.astype(BF16)

    pl.semaphore_wait(barrier, N_PT - 1 + rank)
    for d in range(1, N_VAR):

        @pl.when(jnp.logical_not(first[d]))
        def _():
            pl.semaphore_signal(z_go.at[N_VAR - 1 - d], inc=1, device_id=above(d), device_id_type=MESH)

    def send_ask(dx, dy, dc):
        other = peer(dx, dy, dc)
        pltpu.make_async_remote_copy(
            src_ref=ask.at[other], dst_ref=asked_v.at[code(dx, dy, dc)], send_sem=q_send, recv_sem=q_recv,
            device_id={"pt": other}, device_id_type=MESH,
        ).start()

    each_offset(send_ask)
    asked_v[N_PT - 1] = ask[me]
    spread = [
        pltpu.make_async_remote_copy(
            src_ref=field.at[pl.ds(level * OWN, OWN)], dst_ref=field.at[pl.ds(level * OWN, OWN)],
            send_sem=z_send.at[d - 1], recv_sem=z_recv.at[d - 1], device_id=above(d), device_id_type=MESH,
        )
        for d in range(1, N_VAR)
    ]
    for d in range(1, N_VAR):

        @pl.when(jnp.logical_not(first[d]))
        def _():
            spread[d - 1].start()

    slip_copy.wait()
    lane16 = lax.broadcasted_iota(jnp.int32, (16, LANES), 1) // 32

    def turn(g, carry):
        for n in range(BLOCKS):
            piece = slip[pl.ds(4 * g, 4), :, LANES * n : LANES * (n + 1)].reshape(LANES, LANES)
            flipped = jnp.transpose(piece)
            for half in range(2):
                rows = [flipped[16 * (4 * half + q) : 16 * (4 * half + q) + 16, :] for q in range(4)]
                for v in range(4):
                    mixed = rows[v]
                    for q in range(4):
                        if q != v:
                            mixed = jnp.where(lane16 == q, pltpu.roll(rows[q], 32 * ((q - v) % 4), 1), mixed)
                    xmat[
                        pl.ds(pl.multiple_of((4 * g + v) * 16, 16), 16),
                        256 * (BLOCKS - 1 - n) + LANES * half : 256 * (BLOCKS - 1 - n) + LANES * (half + 1),
                    ] = mixed
        return carry

    lax.fori_loop(0, 4, turn, 0)

    for d in range(1, N_VAR):

        @pl.when(first[d])
        def _():
            pl.semaphore_wait(z_go.at[d - 1], 1)
            spread[d - 1].start()

    everyone = pltpu.make_async_remote_copy(
        src_ref=ask.at[pl.ds(0, N_PT - 1)], dst_ref=asked_v.at[pl.ds(0, N_PT - 1)], send_sem=q_send, recv_sem=q_recv,
        device_id=sibling, device_id_type=MESH,
    )
    everyone.wait_recv()
    compact[...] = jnp.sum(asked_v[...], axis=0)
    to_scalar = pltpu.make_async_copy(compact, asked, ask_sem)
    to_scalar.start()
    for d in range(1, N_VAR):
        source = lax.rem(level + (N_VAR - d), N_VAR)
        pltpu.make_async_remote_copy(
            src_ref=field.at[pl.ds(level * OWN, OWN)], dst_ref=field.at[pl.ds(source * OWN, OWN)],
            send_sem=z_send.at[d - 1], recv_sem=z_recv.at[d - 1], device_id=above(d), device_id_type=MESH,
        ).wait_recv()

    to_scalar.wait()

    def answer(where):
        points = [field[asked[0, 2 * where + slot]].astype(F32) for slot in range(2)]
        return [
            jnp.concatenate([point[8 * half : 8 * half + 8] for point in points], axis=0).astype(BF16)
            for half in range(2)
        ]

    inbox = [inbox_0, inbox_1]

    def send_box(half, dx, dy, dc):
        place = code(dx, dy, dc)
        pltpu.make_async_remote_copy(
            src_ref=outbox.at[half, place], dst_ref=inbox[half].at[place], send_sem=g_send.at[half],
            recv_sem=g_recv.at[half], device_id={"pt": peer(dx, dy, dc)}, device_id_type=MESH,
        ).start()

    def serve(dx, dy, dc):
        place = code(dx, dy, dc)
        outbox[0, place], outbox[1, place] = answer(code(-dx % 4, -dy % 4, dc))
        send_box(0, dx, dy, dc)

    each_offset(serve)
    each_offset(functools.partial(send_box, 1))
    inbox_0[N_PT - 1], inbox_1[N_PT - 1] = answer(N_PT - 1)
    for half in range(2):
        inbox[half][N_PT] = jnp.zeros((16, LANES), BF16)
    boxes = [
        pltpu.make_async_remote_copy(
            src_ref=outbox.at[half], dst_ref=inbox[half].at[pl.ds(0, N_PT - 1)],
            send_sem=g_send.at[half], recv_sem=g_recv.at[half], device_id=sibling, device_id_type=MESH,
        )
        for half in range(2)
    ]
    everyone.wait_send()
    for copy in spread:
        copy.wait_send()

    lane32 = lax.broadcasted_iota(jnp.int32, (HELD, LANES), 1)
    wide = lax.broadcasted_iota(jnp.int32, (VARS, 2 * LANES), 1) % LANES
    group8 = lax.broadcasted_iota(jnp.int32, (8, LANES), 1) // 32

    def delay(half, before):
        for r in range(HELD):
            both = inbox[half][pick_s[r]].astype(F32)
            gathered[8 * r : 8 * r + 8, :] = jnp.where(second_s[r] == 1, both[8:], both[:8])
        last = []
        for h in range(2):
            previous = before[h]
            for m in range(4 * half, 4 * half + 4):
                here = gathered[pl.ds(4 * h + m % 4, HELD, stride=8), :].astype(BF16)
                for c in range(BLOCKS):
                    if c == 0:
                        delayed = here
                    else:
                        delayed = jnp.where(
                            lane32 >= 16 * c, pltpu.roll(here, 16 * c, 1), pltpu.roll(previous, 16 * c, 1)
                        )
                    gmat[256 * m + 32 * c : 256 * m + 32 * c + 32, LANES * h : LANES * (h + 1)] = delayed
                previous = here
            last.append(previous)
        return last

    def product(m, first, last):
        start = 256 * (BLOCKS - 1 - m + first)
        return jnp.dot(
            xmat[:, start : start + 256 * (last - first)], gmat[256 * first : 256 * last, :], preferred_element_type=F32
        )

    def finish(m, spill):
        total = spill
        spill = jnp.zeros((VARS, 2 * LANES), F32)
        for f in range(16):
            rows = [zmat[m, h, pl.ds(f, VARS, stride=16), :] for h in range(2)]
            if f == 0:
                total = total + jnp.concatenate(rows, axis=1)
            else:
                rolled = jnp.concatenate([pltpu.roll(rows[h], f, 1) for h in range(2)], axis=1)
                kept = jnp.where(wide >= f, rolled, 0.0)
                total = total + kept
                spill = spill + (rolled - kept)
        quarters = [total[8 * (q // 2) : 8 * (q // 2) + 8, LANES * (q % 2) : LANES * (q % 2) + LANES] for q in range(4)]
        for t in range(4):
            mixed = quarters[t]
            for q in range(4):
                if q != t:
                    mixed = jnp.where(group8 == q, pltpu.roll(quarters[q], 32 * ((q - t) % 4), 1), mixed)
            part[4 * m + t] = mixed
        return spill

    def hand_out(x):
        base = 8 * lax.rem(x + 4 - at_x, 4)

        def give(dy, dc):
            other = 8 * x + 2 * ys[dy] + cs[dc]
            pltpu.make_async_remote_copy(
                src_ref=part.at[other], dst_ref=landed.at[base + 2 * dy + dc - 1], send_sem=y_send, recv_sem=y_recv,
                device_id={"pt": other}, device_id_type=MESH,
            ).start()

        for dy, dc in [(2, 0), (2, 1), (1, 0), (1, 1), (3, 0), (3, 1), (0, 1)]:
            give(dy, dc)

        @pl.when(base > 0)
        def _():
            give(0, 0)

    boxes[0].wait_recv()
    last = delay(0, [jnp.zeros((HELD, LANES), BF16)] * 2)
    spill = jnp.zeros((VARS, 2 * LANES), F32)
    for m in range(BLOCKS):
        whole = product(m, 0, min(m + 1, 4))
        zmat[m, 0] = whole[:, :LANES]
        zmat[m, 1] = whole[:, LANES:]
        if m < 4:
            spill = finish(m, spill)
        if m in (1, 3):
            hand_out(m // 2)

    boxes[1].wait_recv()
    delay(1, last)
    for m in range(4, BLOCKS):
        rest = product(m, 4, m + 1)
        zmat[m, 0] += rest[:, :LANES]
        zmat[m, 1] += rest[:, LANES:]
        spill = finish(m, spill)
    hand_out(3)
    hand_out(2)
    mine = part[me]
    parts = pltpu.make_async_remote_copy(
        src_ref=part.at[pl.ds(0, N_PT - 1)], dst_ref=landed, send_sem=y_send, recv_sem=y_recv,
        device_id=sibling, device_id_type=MESH,
    )
    for copy in boxes:
        copy.wait_send()
    parts.wait_recv()
    mine = mine + jnp.sum(landed[...], axis=0)
    for q in range(4):
        out_ref[8 * (q // 2) : 8 * (q // 2) + 8, q % 2, :] = mine[:, 32 * q : 32 * q + 32]
    parts.wait_send()


def on_device(green_tensor, moment, slip_rate, owner_shard, point_slot, live_counts):
    hbm = pl.BlockSpec(memory_space=pltpu.HBM)
    vmem = pl.BlockSpec(memory_space=pltpu.VMEM)
    dma = pltpu.SemaphoreType.DMA
    length = slip_rate.shape[2]
    in_hbm = [
        pltpu.with_memory_space_constraint(a, pltpu.HBM)
        for a in (slip_rate, green_tensor.reshape(96, length), moment, owner_shard.reshape(1, HELD), point_slot)
    ]
    return pl.pallas_call(
        kernel,
        out_shape=jax.ShapeDtypeStruct((VARS, 2, 32), F32),
        in_specs=[hbm] * 5 + [pl.BlockSpec(memory_space=pltpu.SMEM)],
        out_specs=vmem,
        scratch_shapes=[
            pltpu.VMEM((VARS, HELD, length), BF16),
            pltpu.VMEM((96, length), BF16),
            pltpu.VMEM(moment.shape, BF16),
            pltpu.SMEM((1, HELD), jnp.int32),
            pltpu.SMEM((HELD,), jnp.int32),
            pltpu.VMEM((LANES, LANES), F32),
            pltpu.VMEM((HELD, 16, LANES), BF16),
            pltpu.VMEM((N_PT, 1, LANES), jnp.int32),
            pltpu.VMEM((N_PT, 1, LANES), jnp.int32),
            pltpu.VMEM((1, LANES), jnp.int32),
            pltpu.SMEM((1, LANES), jnp.int32),
            pltpu.SMEM((HELD,), jnp.int32),
            pltpu.SMEM((HELD,), jnp.int32),
            pltpu.VMEM((2, N_PT - 1, 16, LANES), BF16),
            pltpu.VMEM((N_PT + 1, 16, LANES), BF16),
            pltpu.VMEM((N_PT + 1, 16, LANES), BF16),
            pltpu.VMEM((HELD * 8, LANES), F32),
            pltpu.VMEM((VARS * 16, 256 * BLOCKS), BF16),
            pltpu.VMEM((256 * BLOCKS, 2 * LANES), BF16),
            pltpu.VMEM((BLOCKS, 2, VARS * 16, LANES), F32),
            pltpu.VMEM((N_PT, 8, LANES), F32),
            pltpu.VMEM((N_PT - 1, 8, LANES), F32),
            dma, dma, dma((3,)), dma, pltpu.SemaphoreType.REGULAR((N_VAR - 1,)), dma((N_VAR - 1,)), dma((N_VAR - 1,)), dma, dma, dma((2,)), dma((2,)), dma, dma,
        ],
        compiler_params=pltpu.CompilerParams(
            collective_id=0, has_side_effects=True, vmem_limit_bytes=32 * 1024 * 1024
        ),
        name="synthesis",
    )(*in_hbm, live_counts)


def solution(mesh):
    in_specs = (
        P(None, None, ("pt", "var"), None),
        P(None, ("pt", "var")),
        P("var", "pt", None),
        P("pt", None),
        P("pt"),
        P("pt"),
    )
    out_specs = P("var", None, "pt")
    return jax.shard_map(on_device, mesh=mesh, in_specs=in_specs, out_specs=out_specs, check_vma=False)
```

```python
import functools

import jax
import jax.numpy as jnp
from jax import lax
from jax.experimental import pallas as pl
from jax.experimental.pallas import tpu as pltpu
from jax.sharding import PartitionSpec as P

F32 = jnp.float32
BF16 = jnp.bfloat16
LANES = 128
N_PT = 32
N_VAR = 4
HELD = 32
OWN = 8
BLOCKS = 8
VARS = 16
MESH = pl.DeviceIdType.MESH


def offsets():
    every = [(dx, dy, dc) for dx in range(4) for dy in range(4) for dc in range(2)]
    return sorted(every[1:], key=lambda d: -(min(d[0], 4 - d[0]) + min(d[1], 4 - d[1])))


def each_offset(body, near_first=False):
    for dx, dy, dc in reversed(offsets()) if near_first else offsets():
        body(dx, dy, dc)


def code(dx, dy, dc):
    return (8 * dx + 2 * dy + dc + N_PT - 1) % N_PT


def rank_of(level):
    return jnp.where(level == 2, 3, jnp.where(level == 3, 2, level))


def request_table(owner_ref, slot_ref, at_x, at_y, at_c):
    row = lax.broadcasted_iota(jnp.int32, (N_PT, LANES), 0)
    lane = lax.broadcasted_iota(jnp.int32, (N_PT, LANES), 1)
    dx = (row // 8 + 4 - at_x) % 4
    dy = (row // 2 + 4 - at_y) % 4
    dc = (row + at_c) % 2
    free = 2 * ((8 * dx + 2 * dy + dc + N_PT - 1) % N_PT)
    table = jnp.zeros((N_PT, LANES), jnp.int32)
    for r in range(HELD):
        hit = row == owner_ref[0, r]
        table = jnp.where(hit & (lane == free), slot_ref[r], table)
        free = free + hit.astype(jnp.int32)
    return table


def kernel(
    slip_hbm, green_hbm, moment_hbm, owner_hbm, slot_hbm, live_ref, out_ref,
    slip, green, moment, owner_ref, slot_ref, fold, field_0, field_1, ask, asked_v, compact, asked, pick_s, second_s, outbox, inbox_0, inbox_1,
    gathered, xmat, gmat, zmat, part, landed,
    slip_sem, green_sem, small_sem, ask_sem, z_go, z_send, z_recv, q_send, q_recv, g_send, g_recv, y_send, y_recv,
):
    me = lax.axis_index("pt")
    level = lax.axis_index("var")
    at_x, at_y, at_c = lax.div(me, 8), lax.rem(lax.div(me, 2), 4), lax.rem(me, 2)

    xs = [lax.rem(at_x + d, 4) for d in range(4)]
    ys = [lax.rem(at_y + d, 4) for d in range(4)]
    cs = [at_c, 1 - at_c]

    def peer(dx, dy, dc):
        return 8 * xs[dx] + 2 * ys[dy] + cs[dc]

    def above(d):
        return {"var": lax.rem(level + d, N_VAR)}

    field = [field_0, field_1]
    sibling = {"pt": peer(0, 0, 1)}

    slip_copy = pltpu.make_async_copy(slip_hbm, slip, slip_sem)
    green_copy = pltpu.make_async_copy(green_hbm, green, green_sem)
    small = [
        pltpu.make_async_copy(source, here, small_sem.at[i])
        for i, (source, here) in enumerate(
            [(owner_hbm, owner_ref), (slot_hbm, slot_ref), (moment_hbm, moment)]
        )
    ]
    for one in small:
        one.start()
    green_copy.start()
    slip_copy.start()

    barrier = pltpu.get_barrier_semaphore()

    def greet(dx, dy, dc):
        pl.semaphore_signal(barrier, inc=1, device_id={"pt": peer(dx, dy, dc)}, device_id_type=MESH)

    each_offset(greet)
    rank = rank_of(level)
    first = [rank < rank_of(lax.rem(level + d, N_VAR)) for d in range(N_VAR)]
    for d in range(1, N_VAR):

        @pl.when(first[d])
        def _():
            pl.semaphore_signal(barrier, inc=1, device_id=above(d), device_id_type=MESH)

    for one in small:
        one.wait()
    table = request_table(owner_ref, slot_ref, at_x, at_y, at_c)
    for o in range(N_PT):
        ask[o] = table[o : o + 1, :]
    seen = jnp.int32(0)
    for r in range(HELD):
        owner = owner_ref[0, r]
        bit = jnp.left_shift(jnp.int32(1), owner)
        second = jnp.where((seen & bit) != 0, 1, 0)
        seen = seen | bit
        place = (
            8 * lax.rem(at_x + 4 - lax.div(owner, 8), 4)
            + 2 * lax.rem(at_y + 4 - lax.rem(lax.div(owner, 2), 4), 4)
            + lax.rem(at_c + lax.rem(owner, 2), 2)
        )
        place = lax.rem(place + N_PT - 1, N_PT)
        pick_s[r] = jnp.where(r < live_ref[0], place, N_PT)
        second_s[r] = second

    green_copy.wait()
    tall = jnp.transpose(moment[...].astype(F32))
    tall = jnp.concatenate([tall, tall], axis=0)
    for m in range(BLOCKS):
        total = jnp.zeros((2 * OWN, LANES), F32)
        for c in range(6):
            total = total + tall[:, c : c + 1] * green[16 * c : 16 * c + 16, LANES * m : LANES * (m + 1)].astype(F32)
        for h in range(2):
            row = OWN * (8 * (m // 4) + 4 * h + m % 4)
            fold[row : row + OWN, :] = total[OWN * h : OWN * h + OWN]
    for half in range(2):
        for q in range(OWN // 2):
            two = [fold[pl.ds(64 * half + 2 * q + i, 8, stride=OWN), :] for i in range(2)]
            field[half][level * (OWN // 2) + q] = jnp.concatenate(two, axis=0).astype(BF16)

    pl.semaphore_wait(barrier, N_PT - 1 + rank)
    for d in range(1, N_VAR):

        @pl.when(jnp.logical_not(first[d]))
        def _():
            pl.semaphore_signal(z_go.at[N_VAR - 1 - d], inc=1, device_id=above(d), device_id_type=MESH)

    def spread(half, d):
        mine = field[half].at[pl.ds(level * (OWN // 2), OWN // 2)]
        return pltpu.make_async_remote_copy(
            src_ref=mine, dst_ref=mine, send_sem=z_send.at[half, d - 1], recv_sem=z_recv.at[half, d - 1],
            device_id=above(d), device_id_type=MESH,
        )

    for half in range(2):
        for d in (2, 1, 3):

            @pl.when(jnp.logical_not(first[d]))
            def _():
                spread(half, d).start()

    def send_ask(dx, dy, dc):
        other = peer(dx, dy, dc)
        pltpu.make_async_remote_copy(
            src_ref=ask.at[other], dst_ref=asked_v.at[code(dx, dy, dc)], send_sem=q_send, recv_sem=q_recv,
            device_id={"pt": other}, device_id_type=MESH,
        ).start()

    each_offset(send_ask)
    asked_v[N_PT - 1] = ask[me]
    slip_copy.wait()
    lane16 = lax.broadcasted_iota(jnp.int32, (16, LANES), 1) // 32

    def turn(g, carry):
        for n in range(BLOCKS):
            piece = slip[pl.ds(4 * g, 4), :, LANES * n : LANES * (n + 1)].reshape(LANES, LANES)
            flipped = jnp.transpose(piece)
            for half in range(2):
                rows = [flipped[16 * (4 * half + q) : 16 * (4 * half + q) + 16, :] for q in range(4)]
                for v in range(4):
                    mixed = rows[v]
                    for q in range(4):
                        if q != v:
                            mixed = jnp.where(lane16 == q, pltpu.roll(rows[q], 32 * ((q - v) % 4), 1), mixed)
                    xmat[
                        pl.ds(pl.multiple_of((4 * g + v) * 16, 16), 16),
                        256 * (BLOCKS - 1 - n) + LANES * half : 256 * (BLOCKS - 1 - n) + LANES * (half + 1),
                    ] = mixed
        return carry

    lax.fori_loop(0, 4, turn, 0)

    for d in range(1, N_VAR):

        @pl.when(first[d])
        def _():
            pl.semaphore_wait(z_go.at[d - 1], 1)
            spread(0, d).start()
            spread(1, d).start()

    everyone = pltpu.make_async_remote_copy(
        src_ref=ask.at[pl.ds(0, N_PT - 1)], dst_ref=asked_v.at[pl.ds(0, N_PT - 1)], send_sem=q_send, recv_sem=q_recv,
        device_id=sibling, device_id_type=MESH,
    )
    everyone.wait_recv()
    compact[...] = jnp.sum(asked_v[...], axis=0)
    to_scalar = pltpu.make_async_copy(compact, asked, ask_sem)
    to_scalar.start()
    to_scalar.wait()

    def answer(half, where):
        rows = []
        for slot in range(2):
            point = asked[0, 2 * where + slot]
            two = field[half][lax.div(point, 2)].astype(F32)
            rows.append(jnp.where(lax.rem(point, 2) == 1, two[8:], two[:8]))
        return jnp.concatenate(rows, axis=0).astype(BF16)

    inbox = [inbox_0, inbox_1]
    for half in range(2):
        for d in range(1, N_VAR):
            theirs = field[half].at[pl.ds(lax.rem(level + (N_VAR - d), N_VAR) * (OWN // 2), OWN // 2)]
            pltpu.make_async_remote_copy(
                src_ref=theirs, dst_ref=theirs, send_sem=z_send.at[half, d - 1], recv_sem=z_recv.at[half, d - 1],
                device_id=above(d), device_id_type=MESH,
            ).wait_recv()

        def serve(dx, dy, dc):
            place = code(dx, dy, dc)
            outbox[half, place] = answer(half, code(-dx % 4, -dy % 4, dc))
            pltpu.make_async_remote_copy(
                src_ref=outbox.at[half, place], dst_ref=inbox[half].at[place], send_sem=g_send.at[half],
                recv_sem=g_recv.at[half], device_id={"pt": peer(dx, dy, dc)}, device_id_type=MESH,
            ).start()

        each_offset(serve)
        inbox[half][N_PT - 1] = answer(half, N_PT - 1)
        inbox[half][N_PT] = jnp.zeros((16, LANES), BF16)
    boxes = [
        pltpu.make_async_remote_copy(
            src_ref=outbox.at[half], dst_ref=inbox[half].at[pl.ds(0, N_PT - 1)],
            send_sem=g_send.at[half], recv_sem=g_recv.at[half], device_id=sibling, device_id_type=MESH,
        )
        for half in range(2)
    ]
    everyone.wait_send()
    for half in range(2):
        for d in range(1, N_VAR):
            spread(half, d).wait_send()

    lane32 = lax.broadcasted_iota(jnp.int32, (HELD, LANES), 1)
    wide = lax.broadcasted_iota(jnp.int32, (VARS, 2 * LANES), 1) % LANES
    group8 = lax.broadcasted_iota(jnp.int32, (8, LANES), 1) // 32

    def delay(half, before):
        for r in range(HELD):
            both = inbox[half][pick_s[r]].astype(F32)
            gathered[8 * r : 8 * r + 8, :] = jnp.where(second_s[r] == 1, both[8:], both[:8])
        last = []
        for h in range(2):
            previous = before[h]
            for m in range(4 * half, 4 * half + 4):
                here = gathered[pl.ds(4 * h + m % 4, HELD, stride=8), :].astype(BF16)
                for c in range(BLOCKS):
                    if c == 0:
                        delayed = here
                    else:
                        delayed = jnp.where(
                            lane32 >= 16 * c, pltpu.roll(here, 16 * c, 1), pltpu.roll(previous, 16 * c, 1)
                        )
                    gmat[256 * m + 32 * c : 256 * m + 32 * c + 32, LANES * h : LANES * (h + 1)] = delayed
                previous = here
            last.append(previous)
        return last

    def product(m, first, last):
        start = 256 * (BLOCKS - 1 - m + first)
        return jnp.dot(
            xmat[:, start : start + 256 * (last - first)], gmat[256 * first : 256 * last, :], preferred_element_type=F32
        )

    def finish(m, spill):
        total = spill
        spill = jnp.zeros((VARS, 2 * LANES), F32)
        for f in range(16):
            rows = [zmat[m, h, pl.ds(f, VARS, stride=16), :] for h in range(2)]
            if f == 0:
                total = total + jnp.concatenate(rows, axis=1)
            else:
                rolled = jnp.concatenate([pltpu.roll(rows[h], f, 1) for h in range(2)], axis=1)
                kept = jnp.where(wide >= f, rolled, 0.0)
                total = total + kept
                spill = spill + (rolled - kept)
        quarters = [total[8 * (q // 2) : 8 * (q // 2) + 8, LANES * (q % 2) : LANES * (q % 2) + LANES] for q in range(4)]
        for t in range(4):
            mixed = quarters[t]
            for q in range(4):
                if q != t:
                    mixed = jnp.where(group8 == q, pltpu.roll(quarters[q], 32 * ((q - t) % 4), 1), mixed)
            part[4 * m + t] = mixed
        return spill

    def hand_out(x):
        base = 8 * lax.rem(x + 4 - at_x, 4)

        def give(dy, dc):
            other = 8 * x + 2 * ys[dy] + cs[dc]
            pltpu.make_async_remote_copy(
                src_ref=part.at[other], dst_ref=landed.at[base + 2 * dy + dc - 1], send_sem=y_send, recv_sem=y_recv,
                device_id={"pt": other}, device_id_type=MESH,
            ).start()

        for dy, dc in [(2, 0), (2, 1), (1, 0), (1, 1), (3, 0), (3, 1), (0, 1)]:
            give(dy, dc)

        @pl.when(base > 0)
        def _():
            give(0, 0)

    boxes[0].wait_recv()
    last = delay(0, [jnp.zeros((HELD, LANES), BF16)] * 2)
    spill = jnp.zeros((VARS, 2 * LANES), F32)
    for m in range(BLOCKS):
        whole = product(m, 0, min(m + 1, 4))
        zmat[m, 0] = whole[:, :LANES]
        zmat[m, 1] = whole[:, LANES:]
        if m < 4:
            spill = finish(m, spill)
        if m in (1, 3):
            hand_out(m // 2)

    boxes[1].wait_recv()
    delay(1, last)
    for m in range(4, BLOCKS):
        rest = product(m, 4, m + 1)
        zmat[m, 0] += rest[:, :LANES]
        zmat[m, 1] += rest[:, LANES:]
        spill = finish(m, spill)
    hand_out(3)
    hand_out(2)
    mine = part[me]
    parts = pltpu.make_async_remote_copy(
        src_ref=part.at[pl.ds(0, N_PT - 1)], dst_ref=landed, send_sem=y_send, recv_sem=y_recv,
        device_id=sibling, device_id_type=MESH,
    )
    for copy in boxes:
        copy.wait_send()
    parts.wait_recv()
    mine = mine + jnp.sum(landed[...], axis=0)
    for q in range(4):
        out_ref[8 * (q // 2) : 8 * (q // 2) + 8, q % 2, :] = mine[:, 32 * q : 32 * q + 32]
    parts.wait_send()


def on_device(green_tensor, moment, slip_rate, owner_shard, point_slot, live_counts):
    hbm = pl.BlockSpec(memory_space=pltpu.HBM)
    vmem = pl.BlockSpec(memory_space=pltpu.VMEM)
    dma = pltpu.SemaphoreType.DMA
    length = slip_rate.shape[2]
    in_hbm = [
        pltpu.with_memory_space_constraint(a, pltpu.HBM)
        for a in (slip_rate, green_tensor.reshape(96, length), moment, owner_shard.reshape(1, HELD), point_slot)
    ]
    return pl.pallas_call(
        kernel,
        out_shape=jax.ShapeDtypeStruct((VARS, 2, 32), F32),
        in_specs=[hbm] * 5 + [pl.BlockSpec(memory_space=pltpu.SMEM)],
        out_specs=vmem,
        scratch_shapes=[
            pltpu.VMEM((VARS, HELD, length), BF16),
            pltpu.VMEM((96, length), BF16),
            pltpu.VMEM(moment.shape, BF16),
            pltpu.SMEM((1, HELD), jnp.int32),
            pltpu.SMEM((HELD,), jnp.int32),
            pltpu.VMEM((LANES, LANES), F32),
            pltpu.VMEM((HELD // 2, 16, LANES), BF16),
            pltpu.VMEM((HELD // 2, 16, LANES), BF16),
            pltpu.VMEM((N_PT, 1, LANES), jnp.int32),
            pltpu.VMEM((N_PT, 1, LANES), jnp.int32),
            pltpu.VMEM((1, LANES), jnp.int32),
            pltpu.SMEM((1, LANES), jnp.int32),
            pltpu.SMEM((HELD,), jnp.int32),
            pltpu.SMEM((HELD,), jnp.int32),
            pltpu.VMEM((2, N_PT - 1, 16, LANES), BF16),
            pltpu.VMEM((N_PT + 1, 16, LANES), BF16),
            pltpu.VMEM((N_PT + 1, 16, LANES), BF16),
            pltpu.VMEM((HELD * 8, LANES), F32),
            pltpu.VMEM((VARS * 16, 256 * BLOCKS), BF16),
            pltpu.VMEM((256 * BLOCKS, 2 * LANES), BF16),
            pltpu.VMEM((BLOCKS, 2, VARS * 16, LANES), F32),
            pltpu.VMEM((N_PT, 8, LANES), F32),
            pltpu.VMEM((N_PT - 1, 8, LANES), F32),
            dma, dma, dma((3,)), dma, pltpu.SemaphoreType.REGULAR((N_VAR - 1,)), dma((2, N_VAR - 1)), dma((2, N_VAR - 1)), dma, dma, dma((2,)), dma((2,)), dma, dma,
        ],
        compiler_params=pltpu.CompilerParams(
            collective_id=0, has_side_effects=True, vmem_limit_bytes=32 * 1024 * 1024
        ),
        name="synthesis",
    )(*in_hbm, live_counts)


def solution(mesh):
    in_specs = (
        P(None, None, ("pt", "var"), None),
        P(None, ("pt", "var")),
        P("var", "pt", None),
        P("pt", None),
        P("pt"),
        P("pt"),
    )
    out_specs = P("var", None, "pt")
    return jax.shard_map(on_device, mesh=mesh, in_specs=in_specs, out_specs=out_specs, check_vma=False)
```

```python
import functools

import jax
import jax.numpy as jnp
from jax import lax
from jax.experimental import pallas as pl
from jax.experimental.pallas import tpu as pltpu
from jax.sharding import PartitionSpec as P

F32 = jnp.float32
BF16 = jnp.bfloat16
LANES = 128
N_PT = 32
N_VAR = 4
HELD = 32
OWN = 8
BLOCKS = 8
VARS = 16
MESH = pl.DeviceIdType.MESH


def offsets():
    every = [(dx, dy, dc) for dx in range(4) for dy in range(4) for dc in range(2)]
    return sorted(every[1:], key=lambda d: -(min(d[0], 4 - d[0]) + min(d[1], 4 - d[1])))


def each_offset(body, near_first=False):
    for dx, dy, dc in reversed(offsets()) if near_first else offsets():
        body(dx, dy, dc)


def code(dx, dy, dc):
    return (8 * dx + 2 * dy + dc + N_PT - 1) % N_PT


def rank_of(level):
    return jnp.where(level == 2, 3, jnp.where(level == 3, 2, level))


def request_table(owner_ref, slot_ref, at_x, at_y, at_c):
    row = lax.broadcasted_iota(jnp.int32, (N_PT, LANES), 0)
    lane = lax.broadcasted_iota(jnp.int32, (N_PT, LANES), 1)
    dx = (row // 8 + 4 - at_x) % 4
    dy = (row // 2 + 4 - at_y) % 4
    dc = (row + at_c) % 2
    free = 2 * ((8 * dx + 2 * dy + dc + N_PT - 1) % N_PT)
    table = jnp.zeros((N_PT, LANES), jnp.int32)
    for r in range(HELD):
        hit = row == owner_ref[0, r]
        table = jnp.where(hit & (lane == free), slot_ref[r], table)
        free = free + hit.astype(jnp.int32)
    return table


def kernel(
    slip_hbm, green_hbm, moment_hbm, owner_hbm, slot_hbm, live_ref, out_ref,
    slip, green, moment, owner_ref, slot_ref, fold, field_0, field_1, ask, asked_v, compact, asked, pick_s, second_s, outbox, inbox_0, inbox_1,
    gathered, xmat, gmat, zmat, part, landed,
    slip_sem, green_sem, small_sem, ask_sem, z_go, z_send, z_recv, q_send, q_recv, g_send, g_recv, y_send, y_recv,
):
    me = lax.axis_index("pt")
    level = lax.axis_index("var")
    at_x, at_y, at_c = lax.div(me, 8), lax.rem(lax.div(me, 2), 4), lax.rem(me, 2)

    xs = [lax.rem(at_x + d, 4) for d in range(4)]
    ys = [lax.rem(at_y + d, 4) for d in range(4)]
    cs = [at_c, 1 - at_c]

    def peer(dx, dy, dc):
        return 8 * xs[dx] + 2 * ys[dy] + cs[dc]

    def above(d):
        return {"var": lax.rem(level + d, N_VAR)}

    field = [field_0, field_1]
    sibling = {"pt": peer(0, 0, 1)}

    slip_copy = pltpu.make_async_copy(slip_hbm, slip, slip_sem)
    green_copy = pltpu.make_async_copy(green_hbm, green, green_sem)
    small = [
        pltpu.make_async_copy(source, here, small_sem.at[i])
        for i, (source, here) in enumerate(
            [(owner_hbm, owner_ref), (slot_hbm, slot_ref), (moment_hbm, moment)]
        )
    ]
    for one in small:
        one.start()
    green_copy.start()
    slip_copy.start()

    barrier = pltpu.get_barrier_semaphore()

    def greet(dx, dy, dc):
        pl.semaphore_signal(barrier, inc=1, device_id={"pt": peer(dx, dy, dc)}, device_id_type=MESH)

    each_offset(greet)
    rank = rank_of(level)
    first = [rank < rank_of(lax.rem(level + d, N_VAR)) for d in range(N_VAR)]
    for d in range(1, N_VAR):

        @pl.when(first[d])
        def _():
            pl.semaphore_signal(barrier, inc=1, device_id=above(d), device_id_type=MESH)

    for one in small:
        one.wait()
    table = request_table(owner_ref, slot_ref, at_x, at_y, at_c)
    for o in range(N_PT):
        ask[o] = table[o : o + 1, :]
    green_copy.wait()
    tall = jnp.transpose(moment[...].astype(F32))
    tall = jnp.concatenate([tall, tall], axis=0)
    for m in range(BLOCKS):
        total = jnp.zeros((2 * OWN, LANES), F32)
        for c in range(6):
            total = total + tall[:, c : c + 1] * green[16 * c : 16 * c + 16, LANES * m : LANES * (m + 1)].astype(F32)
        for h in range(2):
            row = OWN * (8 * (m // 4) + 4 * h + m % 4)
            fold[row : row + OWN, :] = total[OWN * h : OWN * h + OWN]
    for half in range(2):
        for q in range(OWN // 2):
            two = [fold[pl.ds(64 * half + 2 * q + i, 8, stride=OWN), :] for i in range(2)]
            field[half][level * (OWN // 2) + q] = jnp.concatenate(two, axis=0).astype(BF16)

    pl.semaphore_wait(barrier, N_PT - 1 + rank)
    for d in range(1, N_VAR):

        @pl.when(jnp.logical_not(first[d]))
        def _():
            pl.semaphore_signal(z_go.at[N_VAR - 1 - d], inc=1, device_id=above(d), device_id_type=MESH)

    def spread(half, d):
        mine = field[half].at[pl.ds(level * (OWN // 2), OWN // 2)]
        return pltpu.make_async_remote_copy(
            src_ref=mine, dst_ref=mine, send_sem=z_send.at[half, d - 1], recv_sem=z_recv.at[half, d - 1],
            device_id=above(d), device_id_type=MESH,
        )

    for half in range(2):
        for d in (2, 1, 3):

            @pl.when(jnp.logical_not(first[d]))
            def _():
                spread(half, d).start()

    def send_ask(dx, dy, dc):
        other = peer(dx, dy, dc)
        pltpu.make_async_remote_copy(
            src_ref=ask.at[other], dst_ref=asked_v.at[code(dx, dy, dc)], send_sem=q_send, recv_sem=q_recv,
            device_id={"pt": other}, device_id_type=MESH,
        ).start()

    each_offset(send_ask)
    asked_v[N_PT - 1] = ask[me]
    seen = jnp.int32(0)
    for r in range(HELD):
        owner = owner_ref[0, r]
        bit = jnp.left_shift(jnp.int32(1), owner)
        second = jnp.where((seen & bit) != 0, 1, 0)
        seen = seen | bit
        place = (
            8 * lax.rem(at_x + 4 - lax.div(owner, 8), 4)
            + 2 * lax.rem(at_y + 4 - lax.rem(lax.div(owner, 2), 4), 4)
            + lax.rem(at_c + lax.rem(owner, 2), 2)
        )
        place = lax.rem(place + N_PT - 1, N_PT)
        pick_s[r] = jnp.where(r < live_ref[0], place, N_PT)
        second_s[r] = second

    slip_copy.wait()
    lane16 = lax.broadcasted_iota(jnp.int32, (16, LANES), 1) // 32

    def turn(g, carry):
        for n in range(BLOCKS):
            piece = slip[pl.ds(4 * g, 4), :, LANES * n : LANES * (n + 1)].reshape(LANES, LANES)
            flipped = jnp.transpose(piece)
            for half in range(2):
                rows = [flipped[16 * (4 * half + q) : 16 * (4 * half + q) + 16, :] for q in range(4)]
                for v in range(4):
                    mixed = rows[v]
                    for q in range(4):
                        if q != v:
                            mixed = jnp.where(lane16 == q, pltpu.roll(rows[q], 32 * ((q - v) % 4), 1), mixed)
                    xmat[
                        pl.ds(pl.multiple_of((4 * g + v) * 16, 16), 16),
                        256 * (BLOCKS - 1 - n) + LANES * half : 256 * (BLOCKS - 1 - n) + LANES * (half + 1),
                    ] = mixed
        return carry

    lax.fori_loop(0, 4, turn, 0)

    for d in range(1, N_VAR):

        @pl.when(first[d])
        def _():
            pl.semaphore_wait(z_go.at[d - 1], 1)
            spread(0, d).start()
            spread(1, d).start()

    everyone = pltpu.make_async_remote_copy(
        src_ref=ask.at[pl.ds(0, N_PT - 1)], dst_ref=asked_v.at[pl.ds(0, N_PT - 1)], send_sem=q_send, recv_sem=q_recv,
        device_id=sibling, device_id_type=MESH,
    )
    everyone.wait_recv()
    compact[...] = jnp.sum(asked_v[...], axis=0)
    to_scalar = pltpu.make_async_copy(compact, asked, ask_sem)
    to_scalar.start()
    to_scalar.wait()

    def answer(half, where):
        rows = []
        for slot in range(2):
            point = asked[0, 2 * where + slot]
            two = field[half][lax.div(point, 2)].astype(F32)
            rows.append(jnp.where(lax.rem(point, 2) == 1, two[8:], two[:8]))
        return jnp.concatenate(rows, axis=0).astype(BF16)

    inbox = [inbox_0, inbox_1]
    for half in range(2):
        for d in range(1, N_VAR):
            theirs = field[half].at[pl.ds(lax.rem(level + (N_VAR - d), N_VAR) * (OWN // 2), OWN // 2)]
            pltpu.make_async_remote_copy(
                src_ref=theirs, dst_ref=theirs, send_sem=z_send.at[half, d - 1], recv_sem=z_recv.at[half, d - 1],
                device_id=above(d), device_id_type=MESH,
            ).wait_recv()

        def serve(dx, dy, dc):
            place = code(dx, dy, dc)
            outbox[half, place] = answer(half, code(-dx % 4, -dy % 4, dc))
            pltpu.make_async_remote_copy(
                src_ref=outbox.at[half, place], dst_ref=inbox[half].at[place], send_sem=g_send.at[half],
                recv_sem=g_recv.at[half], device_id={"pt": peer(dx, dy, dc)}, device_id_type=MESH,
            ).start()

        each_offset(serve)
        inbox[half][N_PT - 1] = answer(half, N_PT - 1)
        inbox[half][N_PT] = jnp.zeros((16, LANES), BF16)
    boxes = [
        pltpu.make_async_remote_copy(
            src_ref=outbox.at[half], dst_ref=inbox[half].at[pl.ds(0, N_PT - 1)],
            send_sem=g_send.at[half], recv_sem=g_recv.at[half], device_id=sibling, device_id_type=MESH,
        )
        for half in range(2)
    ]
    everyone.wait_send()
    for half in range(2):
        for d in range(1, N_VAR):
            spread(half, d).wait_send()

    lane32 = lax.broadcasted_iota(jnp.int32, (HELD, LANES), 1)
    wide = lax.broadcasted_iota(jnp.int32, (VARS, 2 * LANES), 1) % LANES
    group8 = lax.broadcasted_iota(jnp.int32, (8, LANES), 1) // 32

    def delay(half, before):
        for r in range(HELD):
            both = inbox[half][pick_s[r]].astype(F32)
            gathered[8 * r : 8 * r + 8, :] = jnp.where(second_s[r] == 1, both[8:], both[:8])
        last = []
        for h in range(2):
            previous = before[h]
            for m in range(4 * half, 4 * half + 4):
                here = gathered[pl.ds(4 * h + m % 4, HELD, stride=8), :].astype(BF16)
                for c in range(BLOCKS):
                    if c == 0:
                        delayed = here
                    else:
                        delayed = jnp.where(
                            lane32 >= 16 * c, pltpu.roll(here, 16 * c, 1), pltpu.roll(previous, 16 * c, 1)
                        )
                    gmat[256 * m + 32 * c : 256 * m + 32 * c + 32, LANES * h : LANES * (h + 1)] = delayed
                previous = here
            last.append(previous)
        return last

    def product(m, first, last):
        start = 256 * (BLOCKS - 1 - m + first)
        return jnp.dot(
            xmat[:, start : start + 256 * (last - first)], gmat[256 * first : 256 * last, :], preferred_element_type=F32
        )

    def finish(m, spill):
        total = spill
        spill = jnp.zeros((VARS, 2 * LANES), F32)
        for f in range(16):
            rows = [zmat[m, h, pl.ds(f, VARS, stride=16), :] for h in range(2)]
            if f == 0:
                total = total + jnp.concatenate(rows, axis=1)
            else:
                rolled = jnp.concatenate([pltpu.roll(rows[h], f, 1) for h in range(2)], axis=1)
                kept = jnp.where(wide >= f, rolled, 0.0)
                total = total + kept
                spill = spill + (rolled - kept)
        quarters = [total[8 * (q // 2) : 8 * (q // 2) + 8, LANES * (q % 2) : LANES * (q % 2) + LANES] for q in range(4)]
        for t in range(4):
            mixed = quarters[t]
            for q in range(4):
                if q != t:
                    mixed = jnp.where(group8 == q, pltpu.roll(quarters[q], 32 * ((q - t) % 4), 1), mixed)
            part[4 * m + t] = mixed
        return spill

    def hand_out(x):
        base = 8 * lax.rem(x + 4 - at_x, 4)

        def give(dy, dc):
            other = 8 * x + 2 * ys[dy] + cs[dc]
            pltpu.make_async_remote_copy(
                src_ref=part.at[other], dst_ref=landed.at[base + 2 * dy + dc - 1], send_sem=y_send, recv_sem=y_recv,
                device_id={"pt": other}, device_id_type=MESH,
            ).start()

        for dy, dc in [(2, 0), (2, 1), (1, 0), (1, 1), (3, 0), (3, 1), (0, 1)]:
            give(dy, dc)

        @pl.when(base > 0)
        def _():
            give(0, 0)

    boxes[0].wait_recv()
    last = delay(0, [jnp.zeros((HELD, LANES), BF16)] * 2)
    spill = jnp.zeros((VARS, 2 * LANES), F32)
    for m in range(BLOCKS):
        whole = product(m, 0, min(m + 1, 4))
        zmat[m, 0] = whole[:, :LANES]
        zmat[m, 1] = whole[:, LANES:]
        if m < 4:
            spill = finish(m, spill)
        if m in (1, 3):
            hand_out(m // 2)

    boxes[1].wait_recv()
    delay(1, last)
    for m in range(4, BLOCKS):
        rest = product(m, 4, m + 1)
        zmat[m, 0] += rest[:, :LANES]
        zmat[m, 1] += rest[:, LANES:]
        spill = finish(m, spill)
    hand_out(3)
    hand_out(2)
    mine = part[me]
    parts = pltpu.make_async_remote_copy(
        src_ref=part.at[pl.ds(0, N_PT - 1)], dst_ref=landed, send_sem=y_send, recv_sem=y_recv,
        device_id=sibling, device_id_type=MESH,
    )
    for copy in boxes:
        copy.wait_send()
    parts.wait_recv()
    mine = mine + jnp.sum(landed[...], axis=0)
    for q in range(4):
        out_ref[8 * (q // 2) : 8 * (q // 2) + 8, q % 2, :] = mine[:, 32 * q : 32 * q + 32]
    parts.wait_send()


def on_device(green_tensor, moment, slip_rate, owner_shard, point_slot, live_counts):
    hbm = pl.BlockSpec(memory_space=pltpu.HBM)
    vmem = pl.BlockSpec(memory_space=pltpu.VMEM)
    dma = pltpu.SemaphoreType.DMA
    length = slip_rate.shape[2]
    in_hbm = [
        pltpu.with_memory_space_constraint(a, pltpu.HBM)
        for a in (slip_rate, green_tensor.reshape(96, length), moment, owner_shard.reshape(1, HELD), point_slot)
    ]
    return pl.pallas_call(
        kernel,
        out_shape=jax.ShapeDtypeStruct((VARS, 2, 32), F32),
        in_specs=[hbm] * 5 + [pl.BlockSpec(memory_space=pltpu.SMEM)],
        out_specs=vmem,
        scratch_shapes=[
            pltpu.VMEM((VARS, HELD, length), BF16),
            pltpu.VMEM((96, length), BF16),
            pltpu.VMEM(moment.shape, BF16),
            pltpu.SMEM((1, HELD), jnp.int32),
            pltpu.SMEM((HELD,), jnp.int32),
            pltpu.VMEM((LANES, LANES), F32),
            pltpu.VMEM((HELD // 2, 16, LANES), BF16),
            pltpu.VMEM((HELD // 2, 16, LANES), BF16),
            pltpu.VMEM((N_PT, 1, LANES), jnp.int32),
            pltpu.VMEM((N_PT, 1, LANES), jnp.int32),
            pltpu.VMEM((1, LANES), jnp.int32),
            pltpu.SMEM((1, LANES), jnp.int32),
            pltpu.SMEM((HELD,), jnp.int32),
            pltpu.SMEM((HELD,), jnp.int32),
            pltpu.VMEM((2, N_PT - 1, 16, LANES), BF16),
            pltpu.VMEM((N_PT + 1, 16, LANES), BF16),
            pltpu.VMEM((N_PT + 1, 16, LANES), BF16),
            pltpu.VMEM((HELD * 8, LANES), F32),
            pltpu.VMEM((VARS * 16, 256 * BLOCKS), BF16),
            pltpu.VMEM((256 * BLOCKS, 2 * LANES), BF16),
            pltpu.VMEM((BLOCKS, 2, VARS * 16, LANES), F32),
            pltpu.VMEM((N_PT, 8, LANES), F32),
            pltpu.VMEM((N_PT - 1, 8, LANES), F32),
            dma, dma, dma((3,)), dma, pltpu.SemaphoreType.REGULAR((N_VAR - 1,)), dma((2, N_VAR - 1)), dma((2, N_VAR - 1)), dma, dma, dma((2,)), dma((2,)), dma, dma,
        ],
        compiler_params=pltpu.CompilerParams(
            collective_id=0, has_side_effects=True, vmem_limit_bytes=32 * 1024 * 1024
        ),
        name="synthesis",
    )(*in_hbm, live_counts)


def solution(mesh):
    in_specs = (
        P(None, None, ("pt", "var"), None),
        P(None, ("pt", "var")),
        P("var", "pt", None),
        P("pt", None),
        P("pt"),
        P("pt"),
    )
    out_specs = P("var", None, "pt")
    return jax.shard_map(on_device, mesh=mesh, in_specs=in_specs, out_specs=out_specs, check_vma=False)
```

```python
import functools

import jax
import jax.numpy as jnp
from jax import lax
from jax.experimental import pallas as pl
from jax.experimental.pallas import tpu as pltpu
from jax.sharding import PartitionSpec as P

F32 = jnp.float32
BF16 = jnp.bfloat16
LANES = 128
N_PT = 32
N_VAR = 4
HELD = 32
OWN = 8
BLOCKS = 8
VARS = 16
MESH = pl.DeviceIdType.MESH


def offsets():
    every = [(dx, dy, dc) for dx in range(4) for dy in range(4) for dc in range(2)]
    return sorted(every[1:], key=lambda d: -(min(d[0], 4 - d[0]) + min(d[1], 4 - d[1])))


def each_offset(body, near_first=False):
    for dx, dy, dc in reversed(offsets()) if near_first else offsets():
        body(dx, dy, dc)


def code(dx, dy, dc):
    return (8 * dx + 2 * dy + dc + N_PT - 1) % N_PT


def rank_of(level):
    return jnp.where(level == 2, 3, jnp.where(level == 3, 2, level))


def request_table(owner_ref, slot_ref, at_x, at_y, at_c):
    row = lax.broadcasted_iota(jnp.int32, (N_PT, LANES), 0)
    lane = lax.broadcasted_iota(jnp.int32, (N_PT, LANES), 1)
    dx = (row // 8 + 4 - at_x) % 4
    dy = (row // 2 + 4 - at_y) % 4
    dc = (row + at_c) % 2
    free = 2 * ((8 * dx + 2 * dy + dc + N_PT - 1) % N_PT)
    table = jnp.zeros((N_PT, LANES), jnp.int32)
    for r in range(HELD):
        hit = row == owner_ref[0, r]
        table = jnp.where(hit & (lane == free), slot_ref[r], table)
        free = free + hit.astype(jnp.int32)
    return table


def kernel(
    slip_hbm, green_hbm, moment_hbm, owner_hbm, slot_hbm, live_ref, out_ref,
    slip, green, moment, owner_ref, slot_ref, fold, field_0, field_1, ask, asked_v, compact, asked, pick_s, second_s, outbox, inbox_0, inbox_1,
    gathered, xmat, gmat, zmat, part, landed,
    slip_sem, green_sem, small_sem, ask_sem, z_go, z_send, z_recv, q_send, q_recv, g_send, g_recv, y_send, y_recv,
):
    me = lax.axis_index("pt")
    level = lax.axis_index("var")
    at_x, at_y, at_c = lax.div(me, 8), lax.rem(lax.div(me, 2), 4), lax.rem(me, 2)

    xs = [lax.rem(at_x + d, 4) for d in range(4)]
    ys = [lax.rem(at_y + d, 4) for d in range(4)]
    cs = [at_c, 1 - at_c]

    def peer(dx, dy, dc):
        return 8 * xs[dx] + 2 * ys[dy] + cs[dc]

    def above(d):
        return {"var": lax.rem(level + d, N_VAR)}

    field = [field_0, field_1]
    sibling = {"pt": peer(0, 0, 1)}

    slip_copy = pltpu.make_async_copy(slip_hbm, slip, slip_sem)
    green_copy = pltpu.make_async_copy(green_hbm, green, green_sem)
    small = [
        pltpu.make_async_copy(source, here, small_sem.at[i])
        for i, (source, here) in enumerate(
            [(owner_hbm, owner_ref), (slot_hbm, slot_ref), (moment_hbm, moment)]
        )
    ]

    barrier = pltpu.get_barrier_semaphore()

    def greet(dx, dy, dc):
        pl.semaphore_signal(barrier, inc=1, device_id={"pt": peer(dx, dy, dc)}, device_id_type=MESH)

    each_offset(greet)
    rank = rank_of(level)
    first = [rank < rank_of(lax.rem(level + d, N_VAR)) for d in range(N_VAR)]
    for d in range(1, N_VAR):

        @pl.when(first[d])
        def _():
            pl.semaphore_signal(barrier, inc=1, device_id=above(d), device_id_type=MESH)

    for one in small:
        one.start()
    green_copy.start()
    slip_copy.start()
    for one in small:
        one.wait()
    table = request_table(owner_ref, slot_ref, at_x, at_y, at_c)
    for o in range(N_PT):
        ask[o] = table[o : o + 1, :]
    seen = jnp.int32(0)
    for r in range(HELD):
        owner = owner_ref[0, r]
        bit = jnp.left_shift(jnp.int32(1), owner)
        second = jnp.where((seen & bit) != 0, 1, 0)
        seen = seen | bit
        place = (
            8 * lax.rem(at_x + 4 - lax.div(owner, 8), 4)
            + 2 * lax.rem(at_y + 4 - lax.rem(lax.div(owner, 2), 4), 4)
            + lax.rem(at_c + lax.rem(owner, 2), 2)
        )
        place = lax.rem(place + N_PT - 1, N_PT)
        pick_s[r] = jnp.where(r < live_ref[0], place, N_PT)
        second_s[r] = second

    green_copy.wait()
    tall = jnp.transpose(moment[...].astype(F32))
    tall = jnp.concatenate([tall, tall], axis=0)
    for m in range(BLOCKS):
        total = jnp.zeros((2 * OWN, LANES), F32)
        for c in range(6):
            total = total + tall[:, c : c + 1] * green[16 * c : 16 * c + 16, LANES * m : LANES * (m + 1)].astype(F32)
        for h in range(2):
            row = OWN * (8 * (m // 4) + 4 * h + m % 4)
            fold[row : row + OWN, :] = total[OWN * h : OWN * h + OWN]
    for half in range(2):
        for q in range(OWN // 2):
            two = [fold[pl.ds(64 * half + 2 * q + i, 8, stride=OWN), :] for i in range(2)]
            field[half][level * (OWN // 2) + q] = jnp.concatenate(two, axis=0).astype(BF16)

    pl.semaphore_wait(barrier, N_PT - 1 + rank)
    for d in range(1, N_VAR):

        @pl.when(jnp.logical_not(first[d]))
        def _():
            pl.semaphore_signal(z_go.at[N_VAR - 1 - d], inc=1, device_id=above(d), device_id_type=MESH)

    def spread(half, d):
        mine = field[half].at[pl.ds(level * (OWN // 2), OWN // 2)]
        return pltpu.make_async_remote_copy(
            src_ref=mine, dst_ref=mine, send_sem=z_send.at[half, d - 1], recv_sem=z_recv.at[half, d - 1],
            device_id=above(d), device_id_type=MESH,
        )

    for half in range(2):
        for d in (2, 1, 3):

            @pl.when(jnp.logical_not(first[d]))
            def _():
                spread(half, d).start()

    def send_ask(dx, dy, dc):
        other = peer(dx, dy, dc)
        pltpu.make_async_remote_copy(
            src_ref=ask.at[other], dst_ref=asked_v.at[code(dx, dy, dc)], send_sem=q_send, recv_sem=q_recv,
            device_id={"pt": other}, device_id_type=MESH,
        ).start()

    each_offset(send_ask)
    asked_v[N_PT - 1] = ask[me]
    slip_copy.wait()
    lane16 = lax.broadcasted_iota(jnp.int32, (16, LANES), 1) // 32

    def turn(g, carry):
        for n in range(BLOCKS):
            piece = slip[pl.ds(4 * g, 4), :, LANES * n : LANES * (n + 1)].reshape(LANES, LANES)
            flipped = jnp.transpose(piece)
            for half in range(2):
                rows = [flipped[16 * (4 * half + q) : 16 * (4 * half + q) + 16, :] for q in range(4)]
                for v in range(4):
                    mixed = rows[v]
                    for q in range(4):
                        if q != v:
                            mixed = jnp.where(lane16 == q, pltpu.roll(rows[q], 32 * ((q - v) % 4), 1), mixed)
                    xmat[
                        pl.ds(pl.multiple_of((4 * g + v) * 16, 16), 16),
                        256 * (BLOCKS - 1 - n) + LANES * half : 256 * (BLOCKS - 1 - n) + LANES * (half + 1),
                    ] = mixed
        return carry

    lax.fori_loop(0, 4, turn, 0)

    for d in range(1, N_VAR):

        @pl.when(first[d])
        def _():
            pl.semaphore_wait(z_go.at[d - 1], 1)
            spread(0, d).start()
            spread(1, d).start()

    everyone = pltpu.make_async_remote_copy(
        src_ref=ask.at[pl.ds(0, N_PT - 1)], dst_ref=asked_v.at[pl.ds(0, N_PT - 1)], send_sem=q_send, recv_sem=q_recv,
        device_id=sibling, device_id_type=MESH,
    )
    everyone.wait_recv()
    compact[...] = jnp.sum(asked_v[...], axis=0)
    to_scalar = pltpu.make_async_copy(compact, asked, ask_sem)
    to_scalar.start()
    to_scalar.wait()

    def answer(half, where):
        rows = []
        for slot in range(2):
            point = asked[0, 2 * where + slot]
            two = field[half][lax.div(point, 2)].astype(F32)
            rows.append(jnp.where(lax.rem(point, 2) == 1, two[8:], two[:8]))
        return jnp.concatenate(rows, axis=0).astype(BF16)

    inbox = [inbox_0, inbox_1]
    for half in range(2):
        for d in range(1, N_VAR):
            theirs = field[half].at[pl.ds(lax.rem(level + (N_VAR - d), N_VAR) * (OWN // 2), OWN // 2)]
            pltpu.make_async_remote_copy(
                src_ref=theirs, dst_ref=theirs, send_sem=z_send.at[half, d - 1], recv_sem=z_recv.at[half, d - 1],
                device_id=above(d), device_id_type=MESH,
            ).wait_recv()

        def serve(dx, dy, dc):
            place = code(dx, dy, dc)
            outbox[half, place] = answer(half, code(-dx % 4, -dy % 4, dc))
            pltpu.make_async_remote_copy(
                src_ref=outbox.at[half, place], dst_ref=inbox[half].at[place], send_sem=g_send.at[half],
                recv_sem=g_recv.at[half], device_id={"pt": peer(dx, dy, dc)}, device_id_type=MESH,
            ).start()

        each_offset(serve)
        inbox[half][N_PT - 1] = answer(half, N_PT - 1)
        inbox[half][N_PT] = jnp.zeros((16, LANES), BF16)
    boxes = [
        pltpu.make_async_remote_copy(
            src_ref=outbox.at[half], dst_ref=inbox[half].at[pl.ds(0, N_PT - 1)],
            send_sem=g_send.at[half], recv_sem=g_recv.at[half], device_id=sibling, device_id_type=MESH,
        )
        for half in range(2)
    ]
    everyone.wait_send()
    for half in range(2):
        for d in range(1, N_VAR):
            spread(half, d).wait_send()

    lane32 = lax.broadcasted_iota(jnp.int32, (HELD, LANES), 1)
    wide = lax.broadcasted_iota(jnp.int32, (VARS, 2 * LANES), 1) % LANES
    group8 = lax.broadcasted_iota(jnp.int32, (8, LANES), 1) // 32

    def delay(half, before):
        for r in range(HELD):
            both = inbox[half][pick_s[r]].astype(F32)
            gathered[8 * r : 8 * r + 8, :] = jnp.where(second_s[r] == 1, both[8:], both[:8])
        last = []
        for h in range(2):
            previous = before[h]
            for m in range(4 * half, 4 * half + 4):
                here = gathered[pl.ds(4 * h + m % 4, HELD, stride=8), :].astype(BF16)
                for c in range(BLOCKS):
                    if c == 0:
                        delayed = here
                    else:
                        delayed = jnp.where(
                            lane32 >= 16 * c, pltpu.roll(here, 16 * c, 1), pltpu.roll(previous, 16 * c, 1)
                        )
                    gmat[256 * m + 32 * c : 256 * m + 32 * c + 32, LANES * h : LANES * (h + 1)] = delayed
                previous = here
            last.append(previous)
        return last

    def product(m, first, last):
        start = 256 * (BLOCKS - 1 - m + first)
        return jnp.dot(
            xmat[:, start : start + 256 * (last - first)], gmat[256 * first : 256 * last, :], preferred_element_type=F32
        )

    def finish(m, spill):
        total = spill
        spill = jnp.zeros((VARS, 2 * LANES), F32)
        for f in range(16):
            rows = [zmat[m, h, pl.ds(f, VARS, stride=16), :] for h in range(2)]
            if f == 0:
                total = total + jnp.concatenate(rows, axis=1)
            else:
                rolled = jnp.concatenate([pltpu.roll(rows[h], f, 1) for h in range(2)], axis=1)
                kept = jnp.where(wide >= f, rolled, 0.0)
                total = total + kept
                spill = spill + (rolled - kept)
        quarters = [total[8 * (q // 2) : 8 * (q // 2) + 8, LANES * (q % 2) : LANES * (q % 2) + LANES] for q in range(4)]
        for t in range(4):
            mixed = quarters[t]
            for q in range(4):
                if q != t:
                    mixed = jnp.where(group8 == q, pltpu.roll(quarters[q], 32 * ((q - t) % 4), 1), mixed)
            part[4 * m + t] = mixed
        return spill

    def hand_out(x):
        base = 8 * lax.rem(x + 4 - at_x, 4)

        def give(dy, dc):
            other = 8 * x + 2 * ys[dy] + cs[dc]
            pltpu.make_async_remote_copy(
                src_ref=part.at[other], dst_ref=landed.at[base + 2 * dy + dc - 1], send_sem=y_send, recv_sem=y_recv,
                device_id={"pt": other}, device_id_type=MESH,
            ).start()

        for dy, dc in [(2, 0), (2, 1), (1, 0), (1, 1), (3, 0), (3, 1), (0, 1)]:
            give(dy, dc)

        @pl.when(base > 0)
        def _():
            give(0, 0)

    boxes[0].wait_recv()
    last = delay(0, [jnp.zeros((HELD, LANES), BF16)] * 2)
    spill = jnp.zeros((VARS, 2 * LANES), F32)
    for m in range(BLOCKS):
        whole = product(m, 0, min(m + 1, 4))
        zmat[m, 0] = whole[:, :LANES]
        zmat[m, 1] = whole[:, LANES:]
        if m < 4:
            spill = finish(m, spill)
        if m in (1, 3):
            hand_out(m // 2)

    boxes[1].wait_recv()
    delay(1, last)
    for m in range(4, BLOCKS):
        rest = product(m, 4, m + 1)
        zmat[m, 0] += rest[:, :LANES]
        zmat[m, 1] += rest[:, LANES:]
        spill = finish(m, spill)
    hand_out(3)
    hand_out(2)
    mine = part[me]
    parts = pltpu.make_async_remote_copy(
        src_ref=part.at[pl.ds(0, N_PT - 1)], dst_ref=landed, send_sem=y_send, recv_sem=y_recv,
        device_id=sibling, device_id_type=MESH,
    )
    for copy in boxes:
        copy.wait_send()
    parts.wait_recv()
    mine = mine + jnp.sum(landed[...], axis=0)
    for q in range(4):
        out_ref[8 * (q // 2) : 8 * (q // 2) + 8, q % 2, :] = mine[:, 32 * q : 32 * q + 32]
    parts.wait_send()


def on_device(green_tensor, moment, slip_rate, owner_shard, point_slot, live_counts):
    hbm = pl.BlockSpec(memory_space=pltpu.HBM)
    vmem = pl.BlockSpec(memory_space=pltpu.VMEM)
    dma = pltpu.SemaphoreType.DMA
    length = slip_rate.shape[2]
    in_hbm = [
        pltpu.with_memory_space_constraint(a, pltpu.HBM)
        for a in (slip_rate, green_tensor.reshape(96, length), moment, owner_shard.reshape(1, HELD), point_slot)
    ]
    return pl.pallas_call(
        kernel,
        out_shape=jax.ShapeDtypeStruct((VARS, 2, 32), F32),
        in_specs=[hbm] * 5 + [pl.BlockSpec(memory_space=pltpu.SMEM)],
        out_specs=vmem,
        scratch_shapes=[
            pltpu.VMEM((VARS, HELD, length), BF16),
            pltpu.VMEM((96, length), BF16),
            pltpu.VMEM(moment.shape, BF16),
            pltpu.SMEM((1, HELD), jnp.int32),
            pltpu.SMEM((HELD,), jnp.int32),
            pltpu.VMEM((LANES, LANES), F32),
            pltpu.VMEM((HELD // 2, 16, LANES), BF16),
            pltpu.VMEM((HELD // 2, 16, LANES), BF16),
            pltpu.VMEM((N_PT, 1, LANES), jnp.int32),
            pltpu.VMEM((N_PT, 1, LANES), jnp.int32),
            pltpu.VMEM((1, LANES), jnp.int32),
            pltpu.SMEM((1, LANES), jnp.int32),
            pltpu.SMEM((HELD,), jnp.int32),
            pltpu.SMEM((HELD,), jnp.int32),
            pltpu.VMEM((2, N_PT - 1, 16, LANES), BF16),
            pltpu.VMEM((N_PT + 1, 16, LANES), BF16),
            pltpu.VMEM((N_PT + 1, 16, LANES), BF16),
            pltpu.VMEM((HELD * 8, LANES), F32),
            pltpu.VMEM((VARS * 16, 256 * BLOCKS), BF16),
            pltpu.VMEM((256 * BLOCKS, 2 * LANES), BF16),
            pltpu.VMEM((BLOCKS, 2, VARS * 16, LANES), F32),
            pltpu.VMEM((N_PT, 8, LANES), F32),
            pltpu.VMEM((N_PT - 1, 8, LANES), F32),
            dma, dma, dma((3,)), dma, pltpu.SemaphoreType.REGULAR((N_VAR - 1,)), dma((2, N_VAR - 1)), dma((2, N_VAR - 1)), dma, dma, dma((2,)), dma((2,)), dma, dma,
        ],
        compiler_params=pltpu.CompilerParams(
            collective_id=0, has_side_effects=True, vmem_limit_bytes=32 * 1024 * 1024
        ),
        name="synthesis",
    )(*in_hbm, live_counts)


def solution(mesh):
    in_specs = (
        P(None, None, ("pt", "var"), None),
        P(None, ("pt", "var")),
        P("var", "pt", None),
        P("pt", None),
        P("pt"),
        P("pt"),
    )
    out_specs = P("var", None, "pt")
    return jax.shard_map(on_device, mesh=mesh, in_specs=in_specs, out_specs=out_specs, check_vma=False)
```
